128 devices in a mesh: prompt: 16 (over z, y), ctx: 8 (over x, core).
Axes of the slice: x: 4, y: 4, z: 4, core: 2. Of those that a mesh axis runs over, the one named last changes fastest.
Arguments:
- probe_vectors: bfloat16 [256, 4, 8192], P('prompt', None, 'ctx'), may hold values from -9.5 to 9.5
- tail_memory_tensor: bfloat16 [256, 512, 2048], P('prompt', None, 'ctx'), may hold values from -6 to 6
- common_lead_memory: bfloat16 [16, 32768, 2048], P('prompt', 'ctx'), may hold values from -6 to 6
- active_rollouts: int32 [16], replicated, may hold values from 4 to 8, as said below
- holder_map: int32 [128], replicated, may hold values from 0 to 15, as said below
- tail_fill_extent: int32 [256], P('prompt'), may hold values from 4 to 512, as said below
Outputs:
- attended: bfloat16 [256, 4, 8192], P('prompt', None, 'ctx')
- log_mass: float32 [256, 4, 64], P('prompt', None, 'ctx')
The draws below stay inside these ranges and needn't reach their ends.
Inputs may be any that keep to these rules, and one draw needn't show every extreme that they name: `active_rollouts`: every prompt keeps at least 4 samples; some prompt keeps all. `holder_map`: each owner index holds at most 16 live samples and at most 4 live samples of one prompt; in every draw some index holds exactly 16 live samples with exactly 4 of one prompt. `tail_fill_extent`: some slot has all 512 positions filled.
All inputs are finite; a program needn't handle non-finite values.
Results may differ from the reference program's by a relative error of at most 0.0057.
Values may be sent and summed in bfloat16 or wider, within the bound.
A program may use at most 192 MiB of HBM per device.

```python
import jax
import jax.numpy as jnp
from jax import lax

QUERY_HEADS = 64
KEY_VALUE_HEADS = 8
HEAD_SIZE = 128
SAMPLE_COUNT = 8
DECODE_STEPS = 4
CAP = 4
PREFIX_PER_PART = 4096
SUFFIX_LENGTH = 512
OWNER_SLOTS = 16
PROMPT_COUNT = 16
PREFIX_LENGTH = 32768
ALL_SUFFIX_SLOTS = 256
N_PROMPT = 16
N_CTX = 8


def shared_direction(key):
    return jax.random.normal(jax.random.fold_in(key, 101), (ALL_SUFFIX_SLOTS, KEY_VALUE_HEADS, HEAD_SIZE), jnp.float32)


def routing_draw(key):
    key = jax.random.fold_in(key, 107)
    first_key, second_key, third_key, fourth_key, fifth_key = jax.random.split(key, 5)
    request_finder = jnp.arange(PROMPT_COUNT, dtype=jnp.int32)
    surviving_total = jax.random.randint(first_key, (PROMPT_COUNT,), CAP, SAMPLE_COUNT + 1)
    full_prompt = jax.random.randint(second_key, (), 0, PROMPT_COUNT)
    surviving_total = jnp.where(request_finder == full_prompt, SAMPLE_COUNT, surviving_total).astype(jnp.int32)
    busy_row = jax.random.randint(third_key, (), 0, PROMPT_COUNT)
    busy_prompts = jax.random.permutation(fourth_key, PROMPT_COUNT)[:OWNER_SLOTS // CAP]
    offsets = jax.random.randint(fifth_key, (PROMPT_COUNT,), 0, PROMPT_COUNT - 1)
    sample_ids = jnp.arange(PROMPT_COUNT * SAMPLE_COUNT, dtype=jnp.int32)
    request_number = sample_ids // SAMPLE_COUNT
    within_offset = sample_ids % SAMPLE_COUNT
    in_busy = jnp.sum((request_number[:, None] == busy_prompts[None, :]).astype(jnp.int32), axis=1) > 0
    is_busy = in_busy & (within_offset < CAP)
    offset_of = jnp.sum(jnp.where(request_number[:, None] == request_finder[None, :], offsets[None, :], 0), axis=1)
    spread = (request_number + offset_of + within_offset) % (PROMPT_COUNT - 1)
    other_row = spread + (spread >= busy_row).astype(jnp.int32)
    holder_map = jnp.where(is_busy, busy_row, other_row).astype(jnp.int32)
    return (surviving_total, holder_map)


def draw_active_rollouts(key, part):
    return routing_draw(key)[0]


def draw_holder_map(key, part):
    return routing_draw(key)[1]


def draw_tail_fill_extent(key, part):
    key = jax.random.fold_in(key, 4)
    first_key, second_key = jax.random.split(key)
    lengths = jax.random.randint(first_key, (ALL_SUFFIX_SLOTS,), DECODE_STEPS, SUFFIX_LENGTH + 1)
    chosen = jax.random.randint(second_key, (), 0, ALL_SUFFIX_SLOTS)
    return jnp.where(jnp.arange(ALL_SUFFIX_SLOTS, dtype=jnp.int32) == chosen, SUFFIX_LENGTH, lengths).astype(jnp.int32)


def draw_probe_vectors(key, part):
    direction = shared_direction(key)
    key = jax.random.fold_in(key, 1)
    group_width = QUERY_HEADS // KEY_VALUE_HEADS
    noise_part = jax.random.normal(key, (ALL_SUFFIX_SLOTS, DECODE_STEPS, QUERY_HEADS, HEAD_SIZE), jnp.float32)
    head_dir = jnp.repeat(direction, group_width, axis=1)
    query_rows = 1.5 * 0.7071 * (head_dir[:, None] + noise_part)
    return jnp.clip(query_rows, -9.5, 9.5).reshape(ALL_SUFFIX_SLOTS, DECODE_STEPS, QUERY_HEADS * HEAD_SIZE).astype(jnp.bfloat16)


def draw_common_lead_memory(key, part):
    key = jax.random.fold_in(key, 2)
    table_entries = jnp.clip(jax.random.normal(key, (PROMPT_COUNT, PREFIX_LENGTH, KEY_VALUE_HEADS, 2, HEAD_SIZE), jnp.float32), -6.0, 6.0)
    return table_entries.reshape(PROMPT_COUNT, PREFIX_LENGTH, KEY_VALUE_HEADS * 2 * HEAD_SIZE).astype(jnp.bfloat16)


def draw_tail_memory_tensor(key, part):
    direction = shared_direction(key)
    key = jax.random.fold_in(key, 3)
    table_entries = jax.random.normal(key, (ALL_SUFFIX_SLOTS, SUFFIX_LENGTH, KEY_VALUE_HEADS, 2, HEAD_SIZE), jnp.float32)
    key_part = table_entries[:, :, :, 0] + 0.3 * direction[:, None]
    table_entries = jnp.stack([key_part, table_entries[:, :, :, 1]], axis=3)
    return jnp.clip(table_entries, -6.0, 6.0).reshape(ALL_SUFFIX_SLOTS, SUFFIX_LENGTH, KEY_VALUE_HEADS * 2 * HEAD_SIZE).astype(jnp.bfloat16)


def setup_inputs(seed: int = 0) -> dict:
    arg_keys = jax.random.split(jax.random.key(seed), 7)
    return {
        "probe_vectors": draw_probe_vectors(jax.random.fold_in(arg_keys[6], 71), 0),
        "tail_memory_tensor": draw_tail_memory_tensor(jax.random.fold_in(arg_keys[6], 71), 0),
        "common_lead_memory": draw_common_lead_memory(jax.random.fold_in(arg_keys[6], 71), 0),
        "active_rollouts": draw_active_rollouts(jax.random.fold_in(arg_keys[6], 71), 0),
        "holder_map": draw_holder_map(jax.random.fold_in(arg_keys[6], 71), 0),
        "tail_fill_extent": draw_tail_fill_extent(jax.random.fold_in(arg_keys[6], 71), 0),
    }


def dispatch_layout(active_rollouts, holder_map):
    sample_ids = jnp.arange(holder_map.shape[0], dtype=jnp.int32)
    request_number = sample_ids // SAMPLE_COUNT
    within_offset = sample_ids % SAMPLE_COUNT
    request_finder = jnp.arange(active_rollouts.shape[0], dtype=jnp.int32)
    surviving_total = jnp.sum(jnp.where(request_number[:, None] == request_finder[None, :], active_rollouts[None, :], 0), axis=1).astype(jnp.int32)
    active_marker = within_offset < surviving_total
    earlier = active_marker[:, None] & (holder_map[:, None] == holder_map[None, :]) & (sample_ids[:, None] < sample_ids[None, :])
    tail_bucket_number = jnp.sum(earlier.astype(jnp.int32), axis=0).astype(jnp.int32)
    same_prompt = earlier & (request_number[:, None] == request_number[None, :])
    worker_ordinal = jnp.sum(same_prompt.astype(jnp.int32), axis=0).astype(jnp.int32)
    return request_number, within_offset, active_marker, tail_bucket_number, worker_ordinal


def prefix_attention(query_head_block, shard_rows):
    head_count = shard_rows.shape[1]
    query_view = query_head_block.reshape(query_head_block.shape[0], head_count, -1, HEAD_SIZE)
    scores = jnp.einsum('rhgd,nhd->hrgn', query_view, shard_rows[:, :, 0], preferred_element_type=jnp.float32) * (HEAD_SIZE ** -0.5)
    highest = jnp.max(scores, axis=-1)
    weights = jnp.exp(scores - highest[..., None])
    totals = jnp.sum(weights, axis=-1)
    values = jnp.einsum('hrgn,nhd->hrgd', weights.astype(jnp.bfloat16), shard_rows[:, :, 1], preferred_element_type=jnp.float32)
    return (values / totals[..., None]).astype(jnp.bfloat16), highest + jnp.log(totals)


def merge_shards(values, lse):
    highest = jnp.max(lse, axis=1, keepdims=True)
    weights = jnp.exp(lse - highest)
    totals = jnp.sum(weights, axis=1)
    merged = jnp.sum(weights[..., None] * values, axis=1) / totals[..., None]
    return merged, highest[:, 0] + jnp.log(totals)


def suffix_attention(query_block, cache_block, lengths):
    slot_count, decode_step_count = query_block.shape[0], query_block.shape[1]
    key_span = cache_block.shape[1]
    head_count = cache_block.shape[2] // (2 * HEAD_SIZE)
    group_width = query_block.shape[2] // (head_count * HEAD_SIZE)
    query_view = query_block.reshape(slot_count, decode_step_count, head_count, group_width, HEAD_SIZE)
    cache_view = cache_block.reshape(slot_count, key_span, head_count, 2, HEAD_SIZE)
    scores = jnp.einsum('sthgd,smhd->sthgm', query_view, cache_view[:, :, :, 0], preferred_element_type=jnp.float32) * (HEAD_SIZE ** -0.5)
    limits = lengths[:, None] - decode_step_count + 1 + jnp.arange(decode_step_count, dtype=jnp.int32)[None, :]
    visible = jnp.arange(key_span, dtype=jnp.int32)[None, None, :] < limits[:, :, None]
    masked = jnp.where(visible[:, :, None, None, :], scores, -1e30)
    highest = jnp.max(masked, axis=-1)
    weights = jnp.exp(masked - highest[..., None])
    totals = jnp.sum(weights, axis=-1)
    values = jnp.einsum('sthgm,smhd->sthgd', weights.astype(jnp.bfloat16), cache_view[:, :, :, 1], preferred_element_type=jnp.float32)
    return values / totals[..., None], highest + jnp.log(totals)


def combine_parts(prefix_output, prefix_log_sum, suffix_output, suffix_log_sum, slot_live):
    log_mass = jnp.logaddexp(prefix_log_sum, suffix_log_sum)
    mixed = jnp.exp(prefix_log_sum - log_mass)[..., None] * prefix_output + jnp.exp(suffix_log_sum - log_mass)[..., None] * suffix_output
    live_mask = slot_live[:, None, None, None]
    attended = (mixed * live_mask[..., None]).astype(jnp.bfloat16)
    row_count, decode_step_count = mixed.shape[0], mixed.shape[1]
    return attended.reshape(row_count, decode_step_count, -1), (log_mass * live_mask).reshape(row_count, decode_step_count, -1)


def reference(probe_vectors, tail_memory_tensor, common_lead_memory, active_rollouts, holder_map, tail_fill_extent):
    group_width = QUERY_HEADS // KEY_VALUE_HEADS
    request_number, within_offset, active_marker, tail_bucket_number, worker_ordinal = dispatch_layout(active_rollouts, holder_map)
    slot_rows = (holder_map * OWNER_SLOTS + jnp.minimum(tail_bucket_number, OWNER_SLOTS - 1)).astype(jnp.int32)
    queries_of_sample = jnp.take(probe_vectors, slot_rows, axis=0)
    samples_each_prompt = queries_of_sample.reshape(PROMPT_COUNT, SAMPLE_COUNT * DECODE_STEPS, KEY_VALUE_HEADS, group_width * HEAD_SIZE)

    def prompt_prefix(pieces):
        query_head_block, prompt_row_block = pieces
        partition_count = prompt_row_block.reshape(N_CTX, PREFIX_PER_PART, KEY_VALUE_HEADS, 2, HEAD_SIZE)

        def shard_part(shard_rows):
            return prefix_attention(query_head_block, shard_rows)

        part_vals, part_lse = lax.map(shard_part, partition_count)
        merged_vals, merged_lse = merge_shards(jnp.moveaxis(part_vals.astype(jnp.float32), 0, 1), jnp.moveaxis(part_lse, 0, 1))
        return merged_vals.astype(jnp.bfloat16), merged_lse

    prefix_output, prefix_log_sum = lax.map(prompt_prefix, (samples_each_prompt, common_lead_memory))
    prefix_output = prefix_output.reshape(PROMPT_COUNT, KEY_VALUE_HEADS, SAMPLE_COUNT, DECODE_STEPS, group_width, HEAD_SIZE)
    prefix_output = jnp.transpose(prefix_output, (0, 2, 3, 1, 4, 5)).reshape(PROMPT_COUNT * SAMPLE_COUNT, DECODE_STEPS, KEY_VALUE_HEADS, group_width, HEAD_SIZE)
    prefix_log_sum = prefix_log_sum.reshape(PROMPT_COUNT, KEY_VALUE_HEADS, SAMPLE_COUNT, DECODE_STEPS, group_width)
    prefix_log_sum = jnp.transpose(prefix_log_sum, (0, 2, 3, 1, 4)).reshape(PROMPT_COUNT * SAMPLE_COUNT, DECODE_STEPS, KEY_VALUE_HEADS, group_width)
    destination = jnp.where(active_marker, holder_map * OWNER_SLOTS + tail_bucket_number, ALL_SUFFIX_SLOTS).astype(jnp.int32)
    slot_output = jnp.zeros((ALL_SUFFIX_SLOTS, DECODE_STEPS, KEY_VALUE_HEADS, group_width, HEAD_SIZE), jnp.float32).at[destination].set(prefix_output.astype(jnp.float32), mode="drop")
    slot_log_sum = jnp.zeros((ALL_SUFFIX_SLOTS, DECODE_STEPS, KEY_VALUE_HEADS, group_width), jnp.float32).at[destination].set(prefix_log_sum, mode="drop")
    slot_live = jnp.zeros((ALL_SUFFIX_SLOTS,), jnp.float32).at[destination].set(jnp.ones((PROMPT_COUNT * SAMPLE_COUNT,), jnp.float32), mode="drop")

    def suffix_of_row(pieces):
        row_queries, row_cache, row_lengths = pieces
        return suffix_attention(row_queries, row_cache, row_lengths)

    suffix_output, suffix_log_sum = lax.map(suffix_of_row, (probe_vectors.reshape(N_PROMPT, OWNER_SLOTS, DECODE_STEPS, QUERY_HEADS * HEAD_SIZE), tail_memory_tensor.reshape(N_PROMPT, OWNER_SLOTS, SUFFIX_LENGTH, KEY_VALUE_HEADS * 2 * HEAD_SIZE), tail_fill_extent.reshape(N_PROMPT, OWNER_SLOTS)))
    suffix_output = suffix_output.reshape(ALL_SUFFIX_SLOTS, DECODE_STEPS, KEY_VALUE_HEADS, group_width, HEAD_SIZE)
    suffix_log_sum = suffix_log_sum.reshape(ALL_SUFFIX_SLOTS, DECODE_STEPS, KEY_VALUE_HEADS, group_width)
    attended, log_mass = combine_parts(slot_output, slot_log_sum, suffix_output, suffix_log_sum, slot_live)
    return attended, log_mass
```

```python
import functools

import jax
import jax.numpy as jnp
from jax import lax
from jax.experimental import pallas as pl
from jax.experimental.pallas import tpu as pltpu
from jax.sharding import PartitionSpec as P

QUERY_HEADS = 64
KEY_VALUE_HEADS = 8
HEAD_SIZE = 128
SAMPLE_COUNT = 8
CAP = 4
OWNER_SLOTS = 16
STEPS = 4
GROUP = QUERY_HEADS // KEY_VALUE_HEADS
WIDTH = GROUP * HEAD_SIZE
PAYLOAD = WIDTH + 128
ROWS = SAMPLE_COUNT * STEPS
SLOT_ROWS = OWNER_SLOTS * STEPS
PAIR_ROWS = CAP * STEPS
CHUNK = 1024
LOG2E = 1.4426950408889634
LN2 = 0.6931471805599453
SCALE = HEAD_SIZE**-0.5 * LOG2E
F32 = jnp.float32
BF16 = jnp.bfloat16
MESH = pl.DeviceIdType.MESH


def iota(shape, dim):
    return lax.broadcasted_iota(jnp.int32, shape, dim)


def one_hot(condition):
    return jnp.where(condition, 1.0, 0.0).astype(F32)


def dot(a, b):
    return jnp.dot(a, b, preferred_element_type=F32)


def dot_rows(a, b):
    return lax.dot_general(a, b, (((1,), (1,)), ((), ())), preferred_element_type=F32)


def layout_vectors(active, holder):
    count = holder.shape[1]
    rows, lanes = iota((count, count), 0), iota((count, count), 1)
    diagonal = rows == lanes
    owner_row = holder.astype(F32)
    owner_col = jnp.sum(jnp.where(diagonal, owner_row, 0.0), axis=1, keepdims=True)
    prompts = active.shape[1]
    in_prompt = iota((count, prompts), 0) // SAMPLE_COUNT == iota((count, prompts), 1)
    kept = jnp.sum(jnp.where(in_prompt, active.astype(F32), 0.0), axis=1, keepdims=True)
    live_col = one_hot((iota((count, 1), 0) % SAMPLE_COUNT).astype(F32) < kept)
    live_row = jnp.sum(jnp.where(diagonal, live_col, 0.0), axis=0, keepdims=True)
    same_owner = owner_col == owner_row
    same_prompt = rows // SAMPLE_COUNT == lanes // SAMPLE_COUNT
    before_row = jnp.where(same_owner & (rows < lanes), live_col, 0.0)
    before_col = jnp.where(same_owner & (lanes < rows), live_row, 0.0)
    slot_row = jnp.sum(before_row, axis=0, keepdims=True)
    slot_col = jnp.sum(before_col, axis=1, keepdims=True)
    ordinal_row = jnp.sum(jnp.where(same_prompt, before_row, 0.0), axis=0, keepdims=True)
    ordinal_col = jnp.sum(jnp.where(same_prompt, before_col, 0.0), axis=1, keepdims=True)
    return (owner_row, live_row, slot_row, ordinal_row), (owner_col, live_col, slot_col, ordinal_col)


def same_step(rows, columns):
    return iota((rows, columns), 0) % STEPS == iota((rows, columns), 1) % STEPS


def split_query(block):
    scaled = block.astype(F32) * SCALE
    high = scaled.astype(BF16)
    low = (scaled - high.astype(F32)).astype(BF16)
    pieces = [
        jnp.concatenate(
            [high[:, g * HEAD_SIZE : (g + 1) * HEAD_SIZE], low[:, g * HEAD_SIZE : (g + 1) * HEAD_SIZE]],
            axis=1,
        )
        for g in range(GROUP)
    ]
    return jnp.concatenate(pieces, axis=0)


def twice(keys):
    return jnp.concatenate([keys, keys], axis=1)


def with_ones(values):
    return jnp.concatenate([values, jnp.ones_like(values)], axis=1)


def by_group_lane(column_blocks, rows, copies):
    lane = iota((rows, 128), 1)
    out = jnp.zeros((rows, 128), F32)
    for g in range(GROUP):
        here = (lane % GROUP == g) & (lane < copies * GROUP)
        out = jnp.where(here, column_blocks[g * rows : (g + 1) * rows, :], out)
    return out


def three_terms(value):
    lane = iota(value.shape, 1)
    high = value.astype(BF16).astype(F32)
    rest = value - high
    middle = rest.astype(BF16).astype(F32)
    low = rest - middle
    out = jnp.where(lane < GROUP, high, jnp.where(lane < 2 * GROUP, middle, low))
    return jnp.where(lane < 3 * GROUP, out, 0.0).astype(BF16)


def sum_terms(terms):
    value = terms.astype(F32)
    return value + pltpu.roll(value, 128 - GROUP, 1) + pltpu.roll(value, 128 - 2 * GROUP, 1)


def spread_terms(value):
    lane = iota(value.shape, 1)
    return jnp.where(
        lane < GROUP,
        value,
        jnp.where(lane < 2 * GROUP, pltpu.roll(value, GROUP, 1), pltpu.roll(value, 2 * GROUP, 1)),
    )


def kernel(
    probes,
    active,
    holder,
    fill,
    tail_hbm,
    lead_hbm,
    out_ref,
    mass_ref,
    tail,
    lead,
    send_q,
    recv_q,
    heads_q,
    part_out,
    part_in,
    ret_out,
    ret_in,
    suffix,
    suffix_lse,
    take_table,
    back_table,
    home_table,
    tail_sem,
    lead_sem,
    q_send,
    q_recv,
    c_send,
    c_recv,
    p_send,
    p_recv,
    r_send,
    r_recv,
):
    row_count = lax.axis_size("prompt")
    ctx_count = lax.axis_size("ctx")
    x_count = ctx_count // 2
    me = lax.axis_index("prompt")
    ctx = lax.axis_index("ctx")
    my_x, my_core = ctx // 2, ctx % 2
    span = lead_hbm.shape[0]
    chunk = min(CHUNK, span)
    pairs = row_count * PAIR_ROWS

    def pair_block(index):
        return pl.ds(pl.multiple_of(index * PAIR_ROWS, PAIR_ROWS), PAIR_ROWS)

    def toward(k):
        x = (my_x + (k + 1) // 2) % x_count
        return x * 2 + (my_core + k) % 2

    def away(k):
        x = (my_x + x_count - ((k + 1) // 2) % x_count) % x_count
        return x * 2 + (my_core + k) % 2

    barrier = pltpu.get_barrier_semaphore()

    def greet_prompt(k, _):
        pl.semaphore_signal(
            barrier, inc=1, device_id={"prompt": (me + k) % row_count}, device_id_type=MESH
        )
        return 0

    def greet_ctx(k, _):
        pl.semaphore_signal(barrier, inc=1, device_id={"ctx": (ctx + k) % ctx_count}, device_id_type=MESH)
        return 0

    lax.fori_loop(1, row_count, greet_prompt, 0)
    lax.fori_loop(1, ctx_count, greet_ctx, 0)

    tail_copy = pltpu.make_async_copy(tail_hbm, tail, tail_sem)
    tail_copy.start()

    def lead_copy(k):
        head = toward(k)
        return pltpu.make_async_copy(
            lead_hbm.at[:, pl.ds(pl.multiple_of(head * 2 * HEAD_SIZE, 2 * HEAD_SIZE), 2 * HEAD_SIZE)],
            lead.at[k],
            lead_sem.at[k],
        )

    def start_lead(k, _):
        lead_copy(k).start()
        return 0

    lax.fori_loop(0, ctx_count, start_lead, 0)

    row_form, col_form = layout_vectors(active[...], holder[...])
    owner_row, live_row, slot_row, ordinal_row = row_form
    owner_col, live_col, slot_col, ordinal_col = col_form
    count = owner_row.shape[1]
    my_row = me.astype(F32)

    pair_of_row = iota((pairs, count), 0) // STEPS
    pair_of_col = iota((count, pairs), 1) // STEPS
    sample_of_lane = iota((pairs, count), 1)
    sample_of_row = iota((count, pairs), 0)
    mine_row = live_row * one_hot(owner_row == my_row)
    to_pair = jnp.where(
        (pair_of_row // CAP == sample_of_lane // SAMPLE_COUNT)
        & ((pair_of_row % CAP).astype(F32) == ordinal_row),
        mine_row,
        0.0,
    )
    from_slot = one_hot((iota((count, SLOT_ROWS), 1) // STEPS).astype(F32) == slot_col)
    send_table = jnp.where(
        same_step(pairs, SLOT_ROWS), dot(to_pair.astype(BF16), from_slot.astype(BF16)), 0.0
    ).astype(BF16)
    packed = dot(send_table, probes[...]).astype(BF16)
    send_q[...] = packed

    pl.semaphore_wait(barrier, row_count - 1 + ctx_count - 1)

    def q_copy(k):
        peer = (me + k) % row_count
        return pltpu.make_async_remote_copy(
            src_ref=send_q.at[pair_block(peer)],
            dst_ref=recv_q.at[pair_block(me)],
            send_sem=q_send.at[k],
            recv_sem=q_recv.at[k],
            device_id={"prompt": peer},
            device_id_type=MESH,
        )

    def start_q(k, _):
        q_copy(k).start()
        return 0

    lax.fori_loop(1, row_count, start_q, 0)
    recv_q[pair_block(me), :] = send_q[pair_block(me), :]

    as_sample = jnp.where(
        (iota((ROWS, count), 1) // SAMPLE_COUNT == me)
        & (iota((ROWS, count), 1) % SAMPLE_COUNT == iota((ROWS, count), 0) // STEPS),
        live_row,
        0.0,
    )
    at_pair = one_hot(
        ((pair_of_col // CAP).astype(F32) == owner_col) & ((pair_of_col % CAP).astype(F32) == ordinal_col)
    )
    take_table[...] = jnp.where(
        same_step(ROWS, pairs), dot(as_sample.astype(BF16), at_pair.astype(BF16)), 0.0
    ).astype(BF16)
    of_pair = one_hot(
        ((pair_of_row // CAP).astype(F32) == owner_row) & ((pair_of_row % CAP).astype(F32) == ordinal_row)
    )
    of_sample = jnp.where(
        (iota((count, ROWS), 0) // SAMPLE_COUNT == me)
        & (iota((count, ROWS), 0) % SAMPLE_COUNT == iota((count, ROWS), 1) // STEPS),
        live_col,
        0.0,
    )
    back_table[...] = jnp.where(
        same_step(pairs, ROWS), dot(of_pair.astype(BF16), of_sample.astype(BF16)), 0.0
    ).astype(BF16)
    mine_col = live_col * one_hot(owner_col == my_row)
    into_slot = one_hot((iota((SLOT_ROWS, count), 0) // STEPS).astype(F32) == slot_row)
    from_pair = jnp.where(
        (pair_of_col // CAP == sample_of_row // SAMPLE_COUNT)
        & ((pair_of_col % CAP).astype(F32) == ordinal_col),
        mine_col,
        0.0,
    )
    home_table[...] = jnp.where(
        same_step(SLOT_ROWS, pairs), dot(into_slot.astype(BF16), from_pair.astype(BF16)), 0.0
    ).astype(BF16)

    tail_copy.wait()
    batch = 4
    block_rows = batch * STEPS
    tail_rows = GROUP * block_rows
    tail_span = tail.shape[1]

    def suffix_group(q, _):
        rows = pl.ds(pl.multiple_of(q * block_rows, block_rows), block_rows)
        query = split_query(probes[rows, :])
        row = iota((tail_rows, 1), 0)
        which = (row // STEPS) % batch
        scores = jnp.zeros((tail_rows, tail_span), F32)
        for s in range(batch):
            found = dot_rows(query, twice(tail[q * batch + s, :, 0:HEAD_SIZE]))
            scores = jnp.where(which == s, found, scores)
        filled = jnp.sum(
            jnp.where(
                iota((tail_rows, OWNER_SLOTS), 1) == q * batch + which, fill[...].astype(F32), 0.0
            ),
            axis=1,
            keepdims=True,
        )
        limit = filled - (STEPS - 1) + (row % STEPS).astype(F32)
        visible = iota((tail_rows, tail_span), 1).astype(F32) < limit
        scores = jnp.where(visible, scores, -1e30)
        highest = jnp.max(scores, axis=1, keepdims=True)
        weights = jnp.exp2(scores - highest).astype(BF16)
        total = jnp.zeros((tail_rows, 2 * HEAD_SIZE), F32)
        for s in range(batch):
            found = dot(weights, with_ones(tail[q * batch + s, :, HEAD_SIZE:]))
            total = jnp.where(which == s, found, total)
        sums = total[:, HEAD_SIZE:]
        values = total[:, :HEAD_SIZE] / sums
        for g in range(GROUP):
            suffix[rows, g * HEAD_SIZE : (g + 1) * HEAD_SIZE] = values[
                g * block_rows : (g + 1) * block_rows, :
            ]
        suffix_lse[rows, :] = by_group_lane(highest + jnp.log2(sums), block_rows, 1)
        return 0

    lax.fori_loop(0, OWNER_SLOTS // batch, suffix_group, 0)

    def wait_q(k, _):
        q_copy(k).wait_recv()
        return 0

    lax.fori_loop(1, row_count, wait_q, 0)
    heads_q[ctx] = dot(take_table[...], recv_q[...]).astype(BF16)

    def c_copy(k):
        return pltpu.make_async_remote_copy(
            src_ref=heads_q.at[ctx],
            dst_ref=heads_q.at[ctx],
            send_sem=c_send.at[k],
            recv_sem=c_recv.at[k],
            device_id={"ctx": away(k)},
            device_id_type=MESH,
        )

    def start_c(k, _):
        c_copy(k).start()
        return 0

    lax.fori_loop(1, ctx_count, start_c, 0)

    def p_copy(k):
        return pltpu.make_async_remote_copy(
            src_ref=part_out.at[k],
            dst_ref=part_in.at[ctx],
            send_sem=p_send.at[k],
            recv_sem=p_recv.at[k],
            device_id={"ctx": toward(k)},
            device_id_type=MESH,
        )

    def prefix_head(k):
        lead_copy(k).wait()
        query = split_query(heads_q[toward(k)])
        rows = query.shape[0]

        def scores_of(i):
            return dot_rows(query, twice(lead[k, i * chunk : (i + 1) * chunk, 0:HEAD_SIZE]))

        highest = jnp.full((rows, 1), -1e30, F32)
        total = jnp.zeros((rows, 2 * HEAD_SIZE), F32)
        scores = scores_of(0)
        for i in range(span // chunk):
            later = scores_of(i + 1) if (i + 1) * chunk < span else None
            top = jnp.maximum(highest, jnp.max(scores, axis=1, keepdims=True))
            weights = jnp.exp2(scores - top).astype(BF16)
            total = total * jnp.exp2(highest - top) + dot(
                weights, with_ones(lead[k, i * chunk : (i + 1) * chunk, HEAD_SIZE:])
            )
            highest, scores = top, later
        sums = total[:, HEAD_SIZE:]
        values = (total[:, :HEAD_SIZE] / sums).astype(BF16)
        for g in range(GROUP):
            part_out[k, :, g * HEAD_SIZE : (g + 1) * HEAD_SIZE] = values[g * ROWS : (g + 1) * ROWS, :]
        part_out[k, :, WIDTH:] = three_terms(by_group_lane(highest + jnp.log2(sums), ROWS, 3))

    prefix_head(0)
    part_in[ctx] = part_out[0]

    def prefix_step(k, _):
        c_copy(k).wait_recv()
        prefix_head(k)
        p_copy(k).start()
        return 0

    lax.fori_loop(1, ctx_count, prefix_step, 0)

    def wait_p(k, _):
        p_copy(k).wait_recv()
        return 0

    lax.fori_loop(1, ctx_count, wait_p, 0)

    masses = [sum_terms(part_in[c, :, WIDTH:]) for c in range(ctx_count)]
    highest = functools.reduce(jnp.maximum, masses)
    shares = [jnp.exp2(mass - highest) for mass in masses]
    whole = functools.reduce(jnp.add, shares)
    shares = [share / whole for share in shares]
    merged = []
    for g in range(GROUP):
        columns = slice(g * HEAD_SIZE, (g + 1) * HEAD_SIZE)
        acc = jnp.zeros((ROWS, HEAD_SIZE), F32)
        for c in range(ctx_count):
            acc = acc + shares[c][:, g : g + 1] * part_in[c, :, columns].astype(F32)
        merged.append(acc.astype(BF16))
    merged.append(three_terms(spread_terms(highest + jnp.log2(whole))))
    ret_out[...] = dot(back_table[...], jnp.concatenate(merged, axis=1)).astype(BF16)

    def r_copy(k):
        peer = (me + k) % row_count
        return pltpu.make_async_remote_copy(
            src_ref=ret_out.at[pair_block(peer)],
            dst_ref=ret_in.at[pair_block(me)],
            send_sem=r_send.at[k],
            recv_sem=r_recv.at[k],
            device_id={"prompt": peer},
            device_id_type=MESH,
        )

    def start_r(k, _):
        r_copy(k).start()
        return 0

    lax.fori_loop(1, row_count, start_r, 0)
    ret_in[pair_block(me), :] = ret_out[pair_block(me), :]

    def wait_sends(k, _):
        q_copy(k).wait_send()
        return 0

    lax.fori_loop(1, row_count, wait_sends, 0)

    def wait_ctx_sends(k, _):
        c_copy(k).wait_send()
        p_copy(k).wait_send()
        return 0

    lax.fori_loop(1, ctx_count, wait_ctx_sends, 0)

    def wait_r(k, _):
        r_copy(k).wait_recv()
        return 0

    lax.fori_loop(1, row_count, wait_r, 0)

    home = dot(home_table[...], ret_in[...])
    alive = jnp.sum(home_table[...].astype(F32), axis=1, keepdims=True)
    prefix_mass = sum_terms(home[:, WIDTH:])
    suffix_mass = suffix_lse[...]
    top = jnp.maximum(prefix_mass, suffix_mass)
    mass = top + jnp.log2(jnp.exp2(prefix_mass - top) + jnp.exp2(suffix_mass - top))
    prefix_share = jnp.exp2(prefix_mass - mass) * alive
    suffix_share = jnp.exp2(suffix_mass - mass) * alive
    for g in range(GROUP):
        columns = slice(g * HEAD_SIZE, (g + 1) * HEAD_SIZE)
        out_ref[:, columns] = (
            prefix_share[:, g : g + 1] * home[:, columns] + suffix_share[:, g : g + 1] * suffix[:, columns]
        ).astype(BF16)
    mass_ref[...] = (mass * (alive * LN2))[:, :GROUP]

    def wait_r_sends(k, _):
        r_copy(k).wait_send()
        return 0

    lax.fori_loop(1, row_count, wait_r_sends, 0)


def per_device(probe_vectors, tail_memory, lead_memory, active_rollouts, holder_map, tail_fill):
    row_count = lax.axis_size("prompt")
    ctx_count = lax.axis_size("ctx")
    slots, steps, width = probe_vectors.shape
    span = lead_memory.shape[1]
    tail_span = tail_memory.shape[1]
    pairs = row_count * PAIR_ROWS
    vmem = pl.BlockSpec(memory_space=pltpu.VMEM)
    anywhere = pl.BlockSpec(memory_space=pl.ANY)
    dma = pltpu.SemaphoreType.DMA
    attended, log_mass = pl.pallas_call(
        kernel,
        out_shape=(
            jax.ShapeDtypeStruct((slots * steps, width), BF16),
            jax.ShapeDtypeStruct((slots * steps, GROUP), F32),
        ),
        in_specs=[vmem, vmem, vmem, vmem, anywhere, anywhere],
        out_specs=(vmem, vmem),
        scratch_shapes=[
            pltpu.VMEM((slots, tail_span, 2 * HEAD_SIZE), BF16),
            pltpu.VMEM((ctx_count, span, 2 * HEAD_SIZE), BF16),
            pltpu.VMEM((pairs, WIDTH), BF16),
            pltpu.VMEM((pairs, WIDTH), BF16),
            pltpu.VMEM((ctx_count, ROWS, WIDTH), BF16),
            pltpu.VMEM((ctx_count, ROWS, PAYLOAD), BF16),
            pltpu.VMEM((ctx_count, ROWS, PAYLOAD), BF16),
            pltpu.VMEM((pairs, PAYLOAD), BF16),
            pltpu.VMEM((pairs, PAYLOAD), BF16),
            pltpu.VMEM((SLOT_ROWS, WIDTH), F32),
            pltpu.VMEM((SLOT_ROWS, 128), F32),
            pltpu.VMEM((ROWS, pairs), BF16),
            pltpu.VMEM((pairs, ROWS), BF16),
            pltpu.VMEM((SLOT_ROWS, pairs), BF16),
            dma,
            dma((ctx_count,)),
            dma((row_count,)),
            dma((row_count,)),
            dma((ctx_count,)),
            dma((ctx_count,)),
            dma((ctx_count,)),
            dma((ctx_count,)),
            dma((row_count,)),
            dma((row_count,)),
        ],
        compiler_params=pltpu.CompilerParams(
            collective_id=0, has_side_effects=True, vmem_limit_bytes=56 * 2**20
        ),
        cost_estimate=pl.CostEstimate(
            flops=5_000_000_000, bytes_accessed=22_000_000, transcendentals=9_000_000
        ),
        name="grouped_attention",
    )(
        probe_vectors.reshape(slots * steps, width),
        active_rollouts.reshape(1, -1),
        holder_map.reshape(1, -1),
        tail_fill.reshape(1, -1),
        tail_memory,
        lead_memory.reshape(span, -1),
    )
    return attended.reshape(slots, steps, width), log_mass.reshape(slots, steps, GROUP)


def solution(mesh):
    return jax.shard_map(
        per_device,
        mesh=mesh,
        in_specs=(
            P("prompt", None, "ctx"),
            P("prompt", None, "ctx"),
            P("prompt", "ctx", None),
            P(),
            P(),
            P("prompt"),
        ),
        out_specs=(P("prompt", None, "ctx"), P("prompt", None, "ctx")),
        check_vma=False,
    )
```

```python
import functools

import jax
import jax.numpy as jnp
from jax import lax
from jax.experimental import pallas as pl
from jax.experimental.pallas import tpu as pltpu
from jax.sharding import PartitionSpec as P

QUERY_HEADS = 64
KEY_VALUE_HEADS = 8
HEAD_SIZE = 128
SAMPLE_COUNT = 8
CAP = 4
OWNER_SLOTS = 16
STEPS = 4
GROUP = QUERY_HEADS // KEY_VALUE_HEADS
WIDTH = GROUP * HEAD_SIZE
PAYLOAD = WIDTH + 128
ROWS = SAMPLE_COUNT * STEPS
SLOT_ROWS = OWNER_SLOTS * STEPS
PAIR_ROWS = CAP * STEPS
CHUNK = 1024
EARLY_GROUPS = 4
LATE_GROUPS = 0
FINISH_STEP = 6
LOG2E = 1.4426950408889634
LN2 = 0.6931471805599453
SCALE = HEAD_SIZE**-0.5 * LOG2E
F32 = jnp.float32
BF16 = jnp.bfloat16
MESH = pl.DeviceIdType.MESH


def iota(shape, dim):
    return lax.broadcasted_iota(jnp.int32, shape, dim)


def one_hot(condition):
    return jnp.where(condition, 1.0, 0.0).astype(F32)


def dot(a, b):
    return jnp.dot(a, b, preferred_element_type=F32)


def dot_rows(a, b):
    return lax.dot_general(a, b, (((1,), (1,)), ((), ())), preferred_element_type=F32)


def layout_vectors(active, holder):
    count = holder.shape[1]
    rows, lanes = iota((count, count), 0), iota((count, count), 1)
    diagonal = rows == lanes
    owner_row = holder.astype(F32)
    owner_col = jnp.sum(jnp.where(diagonal, owner_row, 0.0), axis=1, keepdims=True)
    prompts = active.shape[1]
    in_prompt = iota((count, prompts), 0) // SAMPLE_COUNT == iota((count, prompts), 1)
    kept = jnp.sum(jnp.where(in_prompt, active.astype(F32), 0.0), axis=1, keepdims=True)
    live_col = one_hot((iota((count, 1), 0) % SAMPLE_COUNT).astype(F32) < kept)
    live_row = jnp.sum(jnp.where(diagonal, live_col, 0.0), axis=0, keepdims=True)
    same_owner = owner_col == owner_row
    same_prompt = rows // SAMPLE_COUNT == lanes // SAMPLE_COUNT
    before_row = jnp.where(same_owner & (rows < lanes), live_col, 0.0)
    before_col = jnp.where(same_owner & (lanes < rows), live_row, 0.0)
    slot_row = jnp.sum(before_row, axis=0, keepdims=True)
    slot_col = jnp.sum(before_col, axis=1, keepdims=True)
    ordinal_row = jnp.sum(jnp.where(same_prompt, before_row, 0.0), axis=0, keepdims=True)
    ordinal_col = jnp.sum(jnp.where(same_prompt, before_col, 0.0), axis=1, keepdims=True)
    return (owner_row, live_row, slot_row, ordinal_row), (owner_col, live_col, slot_col, ordinal_col)


def same_step(rows, columns):
    return iota((rows, columns), 0) % STEPS == iota((rows, columns), 1) % STEPS


def split_query(block):
    scaled = block.astype(F32) * SCALE
    high = scaled.astype(BF16)
    low = (scaled - high.astype(F32)).astype(BF16)
    pieces = [
        jnp.concatenate(
            [high[:, g * HEAD_SIZE : (g + 1) * HEAD_SIZE], low[:, g * HEAD_SIZE : (g + 1) * HEAD_SIZE]],
            axis=1,
        )
        for g in range(GROUP)
    ]
    return jnp.concatenate(pieces, axis=0)


def twice(keys):
    return jnp.concatenate([keys, keys], axis=1)


def with_ones(values):
    return jnp.concatenate([values, jnp.ones_like(values)], axis=1)


def by_group_lane(column_blocks, rows, copies):
    lane = iota((rows, 128), 1)
    out = jnp.zeros((rows, 128), F32)
    for g in range(GROUP):
        here = (lane % GROUP == g) & (lane < copies * GROUP)
        out = jnp.where(here, column_blocks[g * rows : (g + 1) * rows, :], out)
    return out


def three_terms(value):
    lane = iota(value.shape, 1)
    high = value.astype(BF16).astype(F32)
    rest = value - high
    middle = rest.astype(BF16).astype(F32)
    low = rest - middle
    out = jnp.where(lane < GROUP, high, jnp.where(lane < 2 * GROUP, middle, low))
    return jnp.where(lane < 3 * GROUP, out, 0.0).astype(BF16)


def sum_terms(terms):
    value = terms.astype(F32)
    return value + pltpu.roll(value, 128 - GROUP, 1) + pltpu.roll(value, 128 - 2 * GROUP, 1)


def spread_terms(value):
    lane = iota(value.shape, 1)
    return jnp.where(
        lane < GROUP,
        value,
        jnp.where(lane < 2 * GROUP, pltpu.roll(value, GROUP, 1), pltpu.roll(value, 2 * GROUP, 1)),
    )


def kernel(
    probes_hbm,
    active_hbm,
    holder_hbm,
    fill_hbm,
    tail_hbm,
    lead_hbm,
    out_ref,
    mass_ref,
    probes,
    active,
    holder,
    fill,
    tail,
    lead,
    queries,
    send_q,
    recv_q,
    heads_q,
    part_out,
    twin_in,
    pair_out,
    pair_in,
    ret_out,
    ret_in,
    suffix,
    suffix_lse,
    take_table,
    back_table,
    home_table,
    small_sem,
    tail_sem,
    lead_sem,
    q_send,
    q_recv,
    c_send,
    c_recv,
    t_send,
    t_recv,
    p_send,
    p_recv,
    r_send,
    r_recv,
):
    row_count = lax.axis_size("prompt")
    ctx_count = lax.axis_size("ctx")
    x_count = ctx_count // 2
    y_count = min(4, row_count)
    z_count = row_count // y_count
    me = lax.axis_index("prompt")
    ctx = lax.axis_index("ctx")
    x, core = ctx // 2, ctx % 2
    z, y = me // y_count, me % y_count
    span = lead_hbm.shape[0]
    chunk = min(CHUNK, span)
    pairs = row_count * PAIR_ROWS

    def ring(a, size):
        return min(a, size - a)

    row_offsets = sorted(
        [(a, b) for a in range(z_count) for b in range(y_count) if a or b],
        key=lambda ab: -ring(ab[0], z_count) - ring(ab[1], y_count),
    )
    ctx_offsets = sorted(
        [(a, b) for a in range(x_count) for b in range(2) if a or b],
        key=lambda ab: -2 * ring(ab[0], x_count) - ab[1],
    )

    def row_peer(offset):
        return ((z + offset[0]) % z_count) * y_count + (y + offset[1]) % y_count

    def ctx_peer(offset):
        return ((x + offset[0]) % x_count) * 2 + (core + offset[1]) % 2

    def pair_block(index):
        return pl.ds(pl.multiple_of(index * PAIR_ROWS, PAIR_ROWS), PAIR_ROWS)

    barrier = pltpu.get_barrier_semaphore()
    for offset in row_offsets:
        pl.semaphore_signal(barrier, inc=1, device_id={"prompt": row_peer(offset)}, device_id_type=MESH)
    for offset in ctx_offsets:
        pl.semaphore_signal(barrier, inc=1, device_id={"ctx": ctx_peer(offset)}, device_id_type=MESH)

    small_copies = [
        pltpu.make_async_copy(source, target, small_sem.at[i])
        for i, (source, target) in enumerate(
            [(active_hbm, active), (holder_hbm, holder), (probes_hbm, probes), (fill_hbm, fill)]
        )
    ]
    for copy in small_copies:
        copy.start()

    def step_x(s):
        return (x + s % x_count + s // x_count) % x_count

    def step_core(s):
        return s // x_count

    def step_head(s):
        return step_x(s) * 2 + step_core(s)

    tail_copy = pltpu.make_async_copy(tail_hbm, tail, tail_sem)
    tail_copy.start()

    def lead_copy(s):
        first = pl.multiple_of(step_head(s) * 2 * HEAD_SIZE, 2 * HEAD_SIZE)
        return pltpu.make_async_copy(
            lead_hbm.at[:, pl.ds(first, 2 * HEAD_SIZE)], lead.at[s], lead_sem.at[s]
        )

    def start_lead(s, _):
        lead_copy(s).start()
        return 0

    lax.fori_loop(0, ctx_count, start_lead, 0)

    for copy in small_copies:
        copy.wait()

    row_form, col_form = layout_vectors(active[...], holder[...])
    owner_row, live_row, slot_row, ordinal_row = row_form
    owner_col, live_col, slot_col, ordinal_col = col_form
    count = owner_row.shape[1]
    my_row = me.astype(F32)

    pair_of_row = iota((pairs, count), 0) // STEPS
    pair_of_col = iota((count, pairs), 1) // STEPS
    sample_of_lane = iota((pairs, count), 1)
    sample_of_row = iota((count, pairs), 0)
    mine_row = live_row * one_hot(owner_row == my_row)
    to_pair = jnp.where(
        (pair_of_row // CAP == sample_of_lane // SAMPLE_COUNT)
        & ((pair_of_row % CAP).astype(F32) == ordinal_row),
        mine_row,
        0.0,
    )
    from_slot = one_hot((iota((count, SLOT_ROWS), 1) // STEPS).astype(F32) == slot_col)
    send_table = jnp.where(
        same_step(pairs, SLOT_ROWS), dot(to_pair.astype(BF16), from_slot.astype(BF16)), 0.0
    ).astype(BF16)
    queries[...] = probes[...].astype(F32).reshape(SLOT_ROWS, WIDTH).astype(BF16)
    send_q[...] = dot(send_table, queries[...]).astype(BF16)

    pl.semaphore_wait(barrier, row_count - 1 + ctx_count - 1)

    def q_copy(i):
        peer = row_peer(row_offsets[i])
        return pltpu.make_async_remote_copy(
            src_ref=send_q.at[pair_block(peer)],
            dst_ref=recv_q.at[pair_block(me)],
            send_sem=q_send.at[i],
            recv_sem=q_recv.at[i],
            device_id={"prompt": peer},
            device_id_type=MESH,
        )

    def start_q():
        for i in range(row_count - 1):
            q_copy(i).start()

    pl.when(core == 0)(start_q)
    recv_q[pair_block(me), :] = send_q[pair_block(me), :]

    as_sample = jnp.where(
        (iota((ROWS, count), 1) // SAMPLE_COUNT == me)
        & (iota((ROWS, count), 1) % SAMPLE_COUNT == iota((ROWS, count), 0) // STEPS),
        live_row,
        0.0,
    )
    at_pair = one_hot(
        ((pair_of_col // CAP).astype(F32) == owner_col) & ((pair_of_col % CAP).astype(F32) == ordinal_col)
    )
    take_table[...] = jnp.where(
        same_step(ROWS, pairs), dot(as_sample.astype(BF16), at_pair.astype(BF16)), 0.0
    ).astype(BF16)
    of_pair = one_hot(
        ((pair_of_row // CAP).astype(F32) == owner_row) & ((pair_of_row % CAP).astype(F32) == ordinal_row)
    )
    of_sample = jnp.where(
        (iota((count, ROWS), 0) // SAMPLE_COUNT == me)
        & (iota((count, ROWS), 0) % SAMPLE_COUNT == iota((count, ROWS), 1) // STEPS),
        live_col,
        0.0,
    )
    back_table[...] = jnp.where(
        same_step(pairs, ROWS), dot(of_pair.astype(BF16), of_sample.astype(BF16)), 0.0
    ).astype(BF16)
    mine_col = live_col * one_hot(owner_col == my_row)
    into_slot = one_hot((iota((SLOT_ROWS, count), 0) // STEPS).astype(F32) == slot_row)
    from_pair = jnp.where(
        (pair_of_col // CAP == sample_of_row // SAMPLE_COUNT)
        & ((pair_of_col % CAP).astype(F32) == ordinal_col),
        mine_col,
        0.0,
    )
    home_table[...] = jnp.where(
        same_step(SLOT_ROWS, pairs), dot(into_slot.astype(BF16), from_pair.astype(BF16)), 0.0
    ).astype(BF16)

    tail_copy.wait()
    batch = 4
    block_rows = batch * STEPS
    tail_rows = GROUP * block_rows
    tail_span = tail.shape[1]

    def suffix_group(q, _):
        rows = pl.ds(pl.multiple_of(q * block_rows, block_rows), block_rows)
        query = split_query(queries[rows, :])
        row = iota((tail_rows, 1), 0)
        which = (row // STEPS) % batch
        scores = jnp.zeros((tail_rows, tail_span), F32)
        for s in range(batch):
            found = dot_rows(query, twice(tail[q * batch + s, :, 0:HEAD_SIZE]))
            scores = jnp.where(which == s, found, scores)
        filled = jnp.sum(
            jnp.where(
                iota((tail_rows, OWNER_SLOTS), 1) == q * batch + which, fill[...].astype(F32), 0.0
            ),
            axis=1,
            keepdims=True,
        )
        limit = filled - (STEPS - 1) + (row % STEPS).astype(F32)
        visible = iota((tail_rows, tail_span), 1).astype(F32) < limit
        scores = jnp.where(visible, scores, -1e30)
        highest = jnp.max(scores, axis=1, keepdims=True)
        weights = jnp.exp2(scores - highest).astype(BF16)
        total = jnp.zeros((tail_rows, 2 * HEAD_SIZE), F32)
        for s in range(batch):
            found = dot(weights, with_ones(tail[q * batch + s, :, HEAD_SIZE:]))
            total = jnp.where(which == s, found, total)
        sums = total[:, HEAD_SIZE:]
        values = total[:, :HEAD_SIZE] / sums
        for g in range(GROUP):
            suffix[rows, g * HEAD_SIZE : (g + 1) * HEAD_SIZE] = values[
                g * block_rows : (g + 1) * block_rows, :
            ]
        suffix_lse[rows, :] = by_group_lane(highest + jnp.log2(sums), block_rows, 1)
        return 0

    groups = OWNER_SLOTS // batch
    lax.fori_loop(0, EARLY_GROUPS, suffix_group, 0)
    pl.when(core == 1)(start_q)
    lax.fori_loop(EARLY_GROUPS, groups - LATE_GROUPS, suffix_group, 0)

    def c_copy(i):
        return pltpu.make_async_remote_copy(
            src_ref=heads_q.at[ctx],
            dst_ref=heads_q.at[ctx],
            send_sem=c_send.at[i],
            recv_sem=c_recv.at[ctx],
            device_id={"ctx": ctx_peer(ctx_offsets[i])},
            device_id_type=MESH,
        )

    def c_arrival(head):
        return pltpu.make_async_remote_copy(
            src_ref=heads_q.at[head],
            dst_ref=heads_q.at[head],
            send_sem=c_send.at[0],
            recv_sem=c_recv.at[head],
            device_id={"ctx": ctx_peer((0, 1))},
            device_id_type=MESH,
        )

    def take_queries():
        for i in range(row_count - 1):
            q_copy(i).wait_recv()
        heads_q[ctx] = dot(take_table[...], recv_q[...]).astype(BF16)
        for i in reversed(range(ctx_count - 1)):
            c_copy(i).start()

    def t_copy(j):
        return pltpu.make_async_remote_copy(
            src_ref=part_out.at[(1 - core) * x_count + j],
            dst_ref=twin_in.at[j],
            send_sem=t_send.at[j],
            recv_sem=t_recv.at[j],
            device_id={"ctx": ctx_peer((0, 1))},
            device_id_type=MESH,
        )

    def p_copy(j):
        return pltpu.make_async_remote_copy(
            src_ref=pair_out.at[j],
            dst_ref=pair_in.at[x],
            send_sem=p_send.at[j],
            recv_sem=p_recv.at[x],
            device_id={"ctx": step_x(core * x_count + j) * 2 + core},
            device_id_type=MESH,
        )

    def p_arrival(offset):
        source = (x + offset) % x_count
        return pltpu.make_async_remote_copy(
            src_ref=pair_out.at[0],
            dst_ref=pair_in.at[source],
            send_sem=p_send.at[0],
            recv_sem=p_recv.at[source],
            device_id={"ctx": source * 2 + core},
            device_id_type=MESH,
        )

    def merge(blocks):
        masses = [sum_terms(block[:, WIDTH:]) for block in blocks]
        highest = functools.reduce(jnp.maximum, masses)
        shares = [jnp.exp2(mass - highest) for mass in masses]
        whole = functools.reduce(jnp.add, shares)
        shares = [share / whole for share in shares]
        merged = []
        for g in range(GROUP):
            columns = slice(g * HEAD_SIZE, (g + 1) * HEAD_SIZE)
            merged.append(
                functools.reduce(
                    jnp.add,
                    [
                        share[:, g : g + 1] * block[:, columns].astype(F32)
                        for share, block in zip(shares, blocks)
                    ],
                ).astype(BF16)
            )
        merged.append(three_terms(spread_terms(highest + jnp.log2(whole))))
        return jnp.concatenate(merged, axis=1)

    def merge_pair(s):
        j = s % x_count
        t_copy(j).wait_recv()
        both = merge([part_out[s], twin_in[j]])

        @pl.when(step_x(s) == x)
        def _():
            pair_in[x] = both

        @pl.when(step_x(s) != x)
        def _():
            pair_out[j] = both
            p_copy(j).start()

    def r_copy(i):
        peer = row_peer(row_offsets[i])
        return pltpu.make_async_remote_copy(
            src_ref=ret_out.at[pair_block(peer)],
            dst_ref=ret_in.at[pair_block(me)],
            send_sem=r_send.at[i],
            recv_sem=r_recv.at[i],
            device_id={"prompt": peer},
            device_id_type=MESH,
        )

    def finish_head():
        for offset in range(1, x_count):
            p_arrival(offset).wait_recv()
        merged = merge([pair_in[i] for i in range(x_count)])
        ret_out[...] = dot(back_table[...], merged).astype(BF16)
        for i in range(row_count - 1):
            r_copy(i).start()
        ret_in[pair_block(me), :] = ret_out[pair_block(me), :]

    def prefix_head(s):
        query = split_query(heads_q[step_head(s)])
        rows = query.shape[0]

        def scores_of(i):
            return dot_rows(query, twice(lead[s, i * chunk : (i + 1) * chunk, 0:HEAD_SIZE]))

        highest = jnp.full((rows, 1), -1e30, F32)
        total = jnp.zeros((rows, 2 * HEAD_SIZE), F32)
        scores = scores_of(0)
        for i in range(span // chunk):
            later = scores_of(i + 1) if (i + 1) * chunk < span else None
            top = jnp.maximum(highest, jnp.max(scores, axis=1, keepdims=True))
            weights = jnp.exp2(scores - top).astype(BF16)
            total = total * jnp.exp2(highest - top) + dot(
                weights, with_ones(lead[s, i * chunk : (i + 1) * chunk, HEAD_SIZE:])
            )
            highest, scores = top, later
        sums = total[:, HEAD_SIZE:]
        values = (total[:, :HEAD_SIZE] / sums).astype(BF16)
        for g in range(GROUP):
            part_out[s, :, g * HEAD_SIZE : (g + 1) * HEAD_SIZE] = values[g * ROWS : (g + 1) * ROWS, :]
        part_out[s, :, WIDTH:] = three_terms(by_group_lane(highest + jnp.log2(sums), ROWS, 3))

    def prefix_step(s, _):
        pl.when(s == core)(take_queries)
        lead_copy(s).wait()

        @pl.when(step_head(s) != ctx)
        def _():
            c_arrival(step_head(s)).wait_recv()

        prefix_head(s)
        j = s % x_count

        @pl.when(step_core(s) != core)
        def _():
            t_copy(j).start()

        merged_step = s - 1 + core

        @pl.when((merged_step >= core * x_count) & (merged_step < (core + 1) * x_count))
        def _():
            merge_pair(merged_step)

        if LATE_GROUPS:

            @pl.when(s == 0)
            def _():
                lax.fori_loop(groups - LATE_GROUPS, groups, suffix_group, 0)

        pl.when(s == FINISH_STEP + (ctx_count - 1 - FINISH_STEP) * core)(finish_head)
        return 0

    lax.fori_loop(0, ctx_count, prefix_step, 0)

    for i in range(row_count - 1):
        q_copy(i).wait_send()
    for i in range(ctx_count - 1):
        c_copy(i).wait_send()
    for j in range(x_count):
        t_copy(j).wait_send()

        @pl.when(step_x(core * x_count + j) != x)
        def _():
            p_copy(j).wait_send()

    for i in range(row_count - 1):
        r_copy(i).wait_recv()

    home = dot(home_table[...], ret_in[...])
    alive = jnp.sum(home_table[...].astype(F32), axis=1, keepdims=True)
    prefix_mass = sum_terms(home[:, WIDTH:])
    suffix_mass = suffix_lse[...]
    top = jnp.maximum(prefix_mass, suffix_mass)
    mass = top + jnp.log2(jnp.exp2(prefix_mass - top) + jnp.exp2(suffix_mass - top))
    prefix_share = jnp.exp2(prefix_mass - mass) * alive
    suffix_share = jnp.exp2(suffix_mass - mass) * alive
    for g in range(GROUP):
        columns = slice(g * HEAD_SIZE, (g + 1) * HEAD_SIZE)
        mixed = (
            prefix_share[:, g : g + 1] * home[:, columns] + suffix_share[:, g : g + 1] * suffix[:, columns]
        )
        out_ref[:, :, columns] = mixed.reshape(OWNER_SLOTS, STEPS, HEAD_SIZE).astype(BF16)
    terms = three_terms(spread_terms(mass * (alive * LN2)))
    by_step = one_hot(
        (iota((SLOT_ROWS, SLOT_ROWS), 0) % STEPS == iota((SLOT_ROWS, SLOT_ROWS), 1) // OWNER_SLOTS)
        & (iota((SLOT_ROWS, SLOT_ROWS), 0) // STEPS == iota((SLOT_ROWS, SLOT_ROWS), 1) % OWNER_SLOTS)
    ).astype(BF16)
    turned = lax.dot_general(terms, by_step, (((0,), (0,)), ((), ())), preferred_element_type=F32)
    turned = turned[:GROUP] + turned[GROUP : 2 * GROUP] + turned[2 * GROUP : 3 * GROUP]
    for t in range(STEPS):
        mass_ref[t] = turned[:, t * OWNER_SLOTS : (t + 1) * OWNER_SLOTS]

    for i in range(row_count - 1):
        r_copy(i).wait_send()


def hand_over(attended, mass, attended_out, mass_out):
    attended_out[...] = attended[...]
    mass_out[...] = mass[...]


def per_device(probe_vectors, tail_memory, lead_memory, active_rollouts, holder_map, tail_fill):
    row_count = lax.axis_size("prompt")
    ctx_count = lax.axis_size("ctx")
    x_count = ctx_count // 2
    slots, steps, width = probe_vectors.shape
    span = lead_memory.shape[1]
    tail_span = tail_memory.shape[1]
    pairs = row_count * PAIR_ROWS
    vmem = pl.BlockSpec(memory_space=pltpu.VMEM)
    anywhere = pl.BlockSpec(memory_space=pl.ANY)
    dma = pltpu.SemaphoreType.DMA
    attended, log_mass = pl.pallas_call(
        kernel,
        out_shape=(
            jax.ShapeDtypeStruct((slots, steps, width), BF16),
            jax.ShapeDtypeStruct((steps, GROUP, slots), F32),
        ),
        in_specs=[anywhere] * 6,
        out_specs=(vmem, vmem),
        scratch_shapes=[
            pltpu.VMEM((slots, steps, width), BF16),
            pltpu.VMEM((1, active_rollouts.shape[0]), jnp.int32),
            pltpu.VMEM((1, holder_map.shape[0]), jnp.int32),
            pltpu.VMEM((1, slots), jnp.int32),
            pltpu.VMEM((slots, tail_span, 2 * HEAD_SIZE), BF16),
            pltpu.VMEM((ctx_count, span, 2 * HEAD_SIZE), BF16),
            pltpu.VMEM((SLOT_ROWS, WIDTH), BF16),
            pltpu.VMEM((pairs, WIDTH), BF16),
            pltpu.VMEM((pairs, WIDTH), BF16),
            pltpu.VMEM((ctx_count, ROWS, WIDTH), BF16),
            pltpu.VMEM((ctx_count, ROWS, PAYLOAD), BF16),
            pltpu.VMEM((x_count, ROWS, PAYLOAD), BF16),
            pltpu.VMEM((x_count, ROWS, PAYLOAD), BF16),
            pltpu.VMEM((x_count, ROWS, PAYLOAD), BF16),
            pltpu.VMEM((pairs, PAYLOAD), BF16),
            pltpu.VMEM((pairs, PAYLOAD), BF16),
            pltpu.VMEM((SLOT_ROWS, WIDTH), F32),
            pltpu.VMEM((SLOT_ROWS, 128), F32),
            pltpu.VMEM((ROWS, pairs), BF16),
            pltpu.VMEM((pairs, ROWS), BF16),
            pltpu.VMEM((SLOT_ROWS, pairs), BF16),
            dma((4,)),
            dma,
            dma((ctx_count,)),
            dma((row_count,)),
            dma((row_count,)),
            dma((ctx_count,)),
            dma((ctx_count,)),
            dma((x_count,)),
            dma((x_count,)),
            dma((x_count,)),
            dma((x_count,)),
            dma((row_count,)),
            dma((row_count,)),
        ],
        compiler_params=pltpu.CompilerParams(
            collective_id=0, has_side_effects=True, vmem_limit_bytes=56 * 2**20
        ),
        cost_estimate=pl.CostEstimate(
            flops=5_000_000_000, bytes_accessed=22_000_000, transcendentals=9_000_000
        ),
        name="grouped_attention",
    )(
        probe_vectors,
        active_rollouts.reshape(1, -1),
        holder_map.reshape(1, -1),
        tail_fill.reshape(1, -1),
        tail_memory,
        lead_memory.reshape(span, -1),
    )
    attended, log_mass = pl.pallas_call(
        hand_over,
        out_shape=(
            jax.ShapeDtypeStruct(attended.shape, attended.dtype),
            jax.ShapeDtypeStruct(log_mass.shape, log_mass.dtype),
        ),
        in_specs=[vmem, vmem],
        out_specs=(vmem, vmem),
        name="hand_over",
    )(attended, log_mass)
    return attended, jnp.transpose(log_mass, (2, 0, 1))


def solution(mesh):
    return jax.shard_map(
        per_device,
        mesh=mesh,
        in_specs=(
            P("prompt", None, "ctx"),
            P("prompt", None, "ctx"),
            P("prompt", "ctx", None),
            P(),
            P(),
            P("prompt"),
        ),
        out_specs=(P("prompt", None, "ctx"), P("prompt", None, "ctx")),
        check_vma=False,
    )
```

```python
import functools

import jax
import jax.numpy as jnp
from jax import lax
from jax.experimental import pallas as pl
from jax.experimental.pallas import tpu as pltpu
from jax.sharding import PartitionSpec as P

QUERY_HEADS = 64
KEY_VALUE_HEADS = 8
HEAD_SIZE = 128
SAMPLE_COUNT = 8
CAP = 4
OWNER_SLOTS = 16
STEPS = 4
GROUP = QUERY_HEADS // KEY_VALUE_HEADS
WIDTH = GROUP * HEAD_SIZE
PAYLOAD = WIDTH + 128
ROWS = SAMPLE_COUNT * STEPS
SLOT_ROWS = OWNER_SLOTS * STEPS
PAIR_ROWS = CAP * STEPS
CHUNK = 1024
EARLY_GROUPS = 3
FINISH_STEP = 6
LOG2E = 1.4426950408889634
LN2 = 0.6931471805599453
SCALE = HEAD_SIZE**-0.5 * LOG2E
F32 = jnp.float32
BF16 = jnp.bfloat16
MESH = pl.DeviceIdType.MESH


def iota(shape, dim):
    return lax.broadcasted_iota(jnp.int32, shape, dim)


def one_hot(condition):
    return jnp.where(condition, 1.0, 0.0).astype(F32)


def dot(a, b):
    return jnp.dot(a, b, preferred_element_type=F32)


def dot_rows(a, b):
    return lax.dot_general(a, b, (((1,), (1,)), ((), ())), preferred_element_type=F32)


def layout_vectors(active, holder):
    count = holder.shape[1]
    rows, lanes = iota((count, count), 0), iota((count, count), 1)
    diagonal = rows == lanes
    owner_row = holder.astype(F32)
    owner_col = jnp.sum(jnp.where(diagonal, owner_row, 0.0), axis=1, keepdims=True)
    prompts = active.shape[1]
    in_prompt = iota((count, prompts), 0) // SAMPLE_COUNT == iota((count, prompts), 1)
    kept = jnp.sum(jnp.where(in_prompt, active.astype(F32), 0.0), axis=1, keepdims=True)
    live_col = one_hot((iota((count, 1), 0) % SAMPLE_COUNT).astype(F32) < kept)
    live_row = jnp.sum(jnp.where(diagonal, live_col, 0.0), axis=0, keepdims=True)
    same_owner = owner_col == owner_row
    same_prompt = rows // SAMPLE_COUNT == lanes // SAMPLE_COUNT
    before_row = jnp.where(same_owner & (rows < lanes), live_col, 0.0)
    before_col = jnp.where(same_owner & (lanes < rows), live_row, 0.0)
    slot_row = jnp.sum(before_row, axis=0, keepdims=True)
    slot_col = jnp.sum(before_col, axis=1, keepdims=True)
    ordinal_row = jnp.sum(jnp.where(same_prompt, before_row, 0.0), axis=0, keepdims=True)
    ordinal_col = jnp.sum(jnp.where(same_prompt, before_col, 0.0), axis=1, keepdims=True)
    return (owner_row, live_row, slot_row, ordinal_row), (owner_col, live_col, slot_col, ordinal_col)


def same_step(rows, columns):
    return iota((rows, columns), 0) % STEPS == iota((rows, columns), 1) % STEPS


def split_query(block):
    scaled = block.astype(F32) * SCALE
    high = scaled.astype(BF16)
    low = (scaled - high.astype(F32)).astype(BF16)
    pieces = [
        jnp.concatenate(
            [high[:, g * HEAD_SIZE : (g + 1) * HEAD_SIZE], low[:, g * HEAD_SIZE : (g + 1) * HEAD_SIZE]],
            axis=1,
        )
        for g in range(GROUP)
    ]
    return jnp.concatenate(pieces, axis=0)


def twice(keys):
    return jnp.concatenate([keys, keys], axis=1)


def with_ones(values):
    return jnp.concatenate([values, jnp.ones_like(values)], axis=1)


def by_group_lane(column_blocks, rows, copies):
    lane = iota((rows, 128), 1)
    out = jnp.zeros((rows, 128), F32)
    for g in range(GROUP):
        here = (lane % GROUP == g) & (lane < copies * GROUP)
        out = jnp.where(here, column_blocks[g * rows : (g + 1) * rows, :], out)
    return out


def three_terms(value):
    lane = iota(value.shape, 1)
    high = value.astype(BF16).astype(F32)
    rest = value - high
    middle = rest.astype(BF16).astype(F32)
    low = rest - middle
    out = jnp.where(lane < GROUP, high, jnp.where(lane < 2 * GROUP, middle, low))
    return jnp.where(lane < 3 * GROUP, out, 0.0).astype(BF16)


def sum_terms(terms):
    value = terms.astype(F32)
    return value + pltpu.roll(value, 128 - GROUP, 1) + pltpu.roll(value, 128 - 2 * GROUP, 1)


def spread_terms(value):
    lane = iota(value.shape, 1)
    return jnp.where(
        lane < GROUP,
        value,
        jnp.where(lane < 2 * GROUP, pltpu.roll(value, GROUP, 1), pltpu.roll(value, 2 * GROUP, 1)),
    )


def kernel(
    probes_hbm,
    active_hbm,
    holder_hbm,
    fill_hbm,
    tail_hbm,
    lead_hbm,
    out_ref,
    mass_ref,
    probes,
    active,
    holder,
    fill,
    tail,
    lead,
    queries,
    send_q,
    recv_q,
    heads_q,
    part_out,
    part_in,
    ret_out,
    ret_in,
    suffix,
    suffix_lse,
    take_table,
    back_table,
    home_table,
    small_sem,
    tail_sem,
    lead_sem,
    q_send,
    q_recv,
    c_send,
    c_recv,
    t_send,
    p_send,
    p_recv,
    r_send,
    r_recv,
):
    row_count = lax.axis_size("prompt")
    ctx_count = lax.axis_size("ctx")
    x_count = ctx_count // 2
    y_count = min(4, row_count)
    z_count = row_count // y_count
    me = lax.axis_index("prompt")
    ctx = lax.axis_index("ctx")
    x, core = lax.div(ctx, 2), lax.rem(ctx, 2)
    z, y = lax.div(me, y_count), lax.rem(me, y_count)
    span = lead_hbm.shape[0]
    chunk = min(CHUNK, span)
    pairs = row_count * PAIR_ROWS

    def ring(a, size):
        return min(a, size - a)

    row_offsets = sorted(
        [(a, b) for a in range(z_count) for b in range(y_count) if a or b],
        key=lambda ab: -ring(ab[0], z_count) - ring(ab[1], y_count),
    )
    ctx_offsets = sorted(
        [(a, b) for a in range(x_count) for b in range(2) if a or b],
        key=lambda ab: -2 * ring(ab[0], x_count) - ab[1],
    )

    def row_peer(offset):
        return lax.rem(z + offset[0], z_count) * y_count + lax.rem(y + offset[1], y_count)

    def ctx_peer(offset):
        return lax.rem(x + offset[0], x_count) * 2 + lax.rem(core + offset[1], 2)

    def pair_block(index):
        return pl.ds(pl.multiple_of(index * PAIR_ROWS, PAIR_ROWS), PAIR_ROWS)

    barrier = pltpu.get_barrier_semaphore()
    for offset in row_offsets:
        pl.semaphore_signal(barrier, inc=1, device_id={"prompt": row_peer(offset)}, device_id_type=MESH)
    for offset in ctx_offsets:
        pl.semaphore_signal(barrier, inc=1, device_id={"ctx": ctx_peer(offset)}, device_id_type=MESH)

    small_copies = [
        pltpu.make_async_copy(source, target, small_sem.at[i])
        for i, (source, target) in enumerate(
            [(active_hbm, active), (holder_hbm, holder), (probes_hbm, probes), (fill_hbm, fill)]
        )
    ]
    for copy in small_copies:
        copy.start()

    def step_x(s):
        return lax.rem(x + lax.rem(s, x_count) + lax.div(s, x_count), x_count)

    def step_core(s):
        return lax.div(s, x_count)

    def step_head(s):
        return step_x(s) * 2 + step_core(s)

    own_step = core * (ctx_count - 1)
    tail_copy = pltpu.make_async_copy(tail_hbm, tail, tail_sem)
    tail_copy.start()

    def lead_copy(s):
        first = pl.multiple_of(step_head(s) * 2 * HEAD_SIZE, 2 * HEAD_SIZE)
        return pltpu.make_async_copy(
            lead_hbm.at[:, pl.ds(first, 2 * HEAD_SIZE)], lead.at[s], lead_sem.at[s]
        )

    def start_lead(s, _):
        lead_copy(s).start()
        return 0

    lax.fori_loop(0, ctx_count, start_lead, 0)

    for copy in small_copies:
        copy.wait()

    row_form, col_form = layout_vectors(active[...], holder[...])
    owner_row, live_row, slot_row, ordinal_row = row_form
    owner_col, live_col, slot_col, ordinal_col = col_form
    count = owner_row.shape[1]
    my_row = me.astype(F32)

    pair_of_row = iota((pairs, count), 0) // STEPS
    pair_of_col = iota((count, pairs), 1) // STEPS
    sample_of_lane = iota((pairs, count), 1)
    sample_of_row = iota((count, pairs), 0)
    mine_row = live_row * one_hot(owner_row == my_row)
    to_pair = jnp.where(
        (pair_of_row // CAP == sample_of_lane // SAMPLE_COUNT)
        & ((pair_of_row % CAP).astype(F32) == ordinal_row),
        mine_row,
        0.0,
    )
    from_slot = one_hot((iota((count, SLOT_ROWS), 1) // STEPS).astype(F32) == slot_col)
    send_table = jnp.where(
        same_step(pairs, SLOT_ROWS), dot(to_pair.astype(BF16), from_slot.astype(BF16)), 0.0
    ).astype(BF16)
    queries[...] = probes[...].astype(F32).reshape(SLOT_ROWS, WIDTH).astype(BF16)
    send_q[...] = dot(send_table, queries[...]).astype(BF16)

    pl.semaphore_wait(barrier, row_count - 1 + ctx_count - 1)

    def q_copy(i):
        peer = row_peer(row_offsets[i])
        return pltpu.make_async_remote_copy(
            src_ref=send_q.at[pair_block(peer)],
            dst_ref=recv_q.at[pair_block(me)],
            send_sem=q_send.at[i],
            recv_sem=q_recv.at[i],
            device_id={"prompt": peer},
            device_id_type=MESH,
        )

    def start_q():
        for i in range(row_count - 1):
            q_copy(i).start()

    pl.when(core == 0)(start_q)
    recv_q[pair_block(me), :] = send_q[pair_block(me), :]

    as_sample = jnp.where(
        (iota((ROWS, count), 1) // SAMPLE_COUNT == me)
        & (iota((ROWS, count), 1) % SAMPLE_COUNT == iota((ROWS, count), 0) // STEPS),
        live_row,
        0.0,
    )
    at_pair = one_hot(
        ((pair_of_col // CAP).astype(F32) == owner_col) & ((pair_of_col % CAP).astype(F32) == ordinal_col)
    )
    take_table[...] = jnp.where(
        same_step(ROWS, pairs), dot(as_sample.astype(BF16), at_pair.astype(BF16)), 0.0
    ).astype(BF16)
    of_pair = one_hot(
        ((pair_of_row // CAP).astype(F32) == owner_row) & ((pair_of_row % CAP).astype(F32) == ordinal_row)
    )
    of_sample = jnp.where(
        (iota((count, ROWS), 0) // SAMPLE_COUNT == me)
        & (iota((count, ROWS), 0) % SAMPLE_COUNT == iota((count, ROWS), 1) // STEPS),
        live_col,
        0.0,
    )
    back_table[...] = jnp.where(
        same_step(pairs, ROWS), dot(of_pair.astype(BF16), of_sample.astype(BF16)), 0.0
    ).astype(BF16)
    mine_col = live_col * one_hot(owner_col == my_row)
    into_slot = one_hot((iota((SLOT_ROWS, count), 0) // STEPS).astype(F32) == slot_row)
    from_pair = jnp.where(
        (pair_of_col // CAP == sample_of_row // SAMPLE_COUNT)
        & ((pair_of_col % CAP).astype(F32) == ordinal_col),
        mine_col,
        0.0,
    )
    home_table[...] = jnp.where(
        same_step(SLOT_ROWS, pairs), dot(into_slot.astype(BF16), from_pair.astype(BF16)), 0.0
    ).astype(BF16)

    tail_copy.wait()
    batch = 4
    block_rows = batch * STEPS
    tail_rows = GROUP * block_rows
    tail_span = tail.shape[1]

    def suffix_group(q, _):
        rows = pl.ds(pl.multiple_of(q * block_rows, block_rows), block_rows)
        query = split_query(queries[rows, :])
        row = iota((tail_rows, 1), 0)
        which = (row // STEPS) % batch
        scores = jnp.zeros((tail_rows, tail_span), F32)
        for s in range(batch):
            found = dot_rows(query, twice(tail[q * batch + s, :, 0:HEAD_SIZE]))
            scores = jnp.where(which == s, found, scores)
        filled = jnp.sum(
            jnp.where(
                iota((tail_rows, OWNER_SLOTS), 1) == q * batch + which, fill[...].astype(F32), 0.0
            ),
            axis=1,
            keepdims=True,
        )
        limit = filled - (STEPS - 1) + (row % STEPS).astype(F32)
        visible = iota((tail_rows, tail_span), 1).astype(F32) < limit
        scores = jnp.where(visible, scores, -1e30)
        highest = jnp.max(scores, axis=1, keepdims=True)
        weights = jnp.exp2(scores - highest).astype(BF16)
        total = jnp.zeros((tail_rows, 2 * HEAD_SIZE), F32)
        for s in range(batch):
            found = dot(weights, with_ones(tail[q * batch + s, :, HEAD_SIZE:]))
            total = jnp.where(which == s, found, total)
        sums = total[:, HEAD_SIZE:]
        values = total[:, :HEAD_SIZE] / sums
        for g in range(GROUP):
            suffix[rows, g * HEAD_SIZE : (g + 1) * HEAD_SIZE] = values[
                g * block_rows : (g + 1) * block_rows, :
            ]
        suffix_lse[rows, :] = by_group_lane(highest + jnp.log2(sums), block_rows, 1)
        return 0

    groups = OWNER_SLOTS // batch
    early = EARLY_GROUPS + (groups - EARLY_GROUPS) * core
    lax.fori_loop(0, early, suffix_group, 0)
    pl.when(core == 1)(start_q)

    near = [(0, 1)] + [(x_count - k, 0) for k in range(1, x_count)]

    def c_copy(i):
        return pltpu.make_async_remote_copy(
            src_ref=heads_q.at[ctx],
            dst_ref=heads_q.at[ctx],
            send_sem=c_send.at[i],
            recv_sem=c_recv.at[ctx],
            device_id={"ctx": ctx_peer(near[i])},
            device_id_type=MESH,
        )

    def twin_copy(head):
        return pltpu.make_async_remote_copy(
            src_ref=heads_q.at[head],
            dst_ref=heads_q.at[head],
            send_sem=t_send.at[head // 2],
            recv_sem=c_recv.at[head],
            device_id={"ctx": ctx_peer((0, 1))},
            device_id_type=MESH,
        )

    def take_queries():
        for i in range(row_count - 1):
            q_copy(i).wait_recv()
        heads_q[ctx] = dot(take_table[...], recv_q[...]).astype(BF16)
        for i in range(len(near)):
            c_copy(i).start()

    def p_copy(s):
        return pltpu.make_async_remote_copy(
            src_ref=part_out.at[s],
            dst_ref=part_in.at[ctx],
            send_sem=p_send.at[s],
            recv_sem=p_recv.at[ctx],
            device_id={"ctx": step_head(s)},
            device_id_type=MESH,
        )

    def p_arrival(source):
        return pltpu.make_async_remote_copy(
            src_ref=part_out.at[0],
            dst_ref=part_in.at[source],
            send_sem=p_send.at[0],
            recv_sem=p_recv.at[source],
            device_id={"ctx": source},
            device_id_type=MESH,
        )

    def merge(blocks):
        masses = [sum_terms(block[:, WIDTH:]) for block in blocks]
        highest = functools.reduce(jnp.maximum, masses)
        shares = [jnp.exp2(mass - highest) for mass in masses]
        whole = functools.reduce(jnp.add, shares)
        shares = [share / whole for share in shares]
        merged = []
        for g in range(GROUP):
            columns = slice(g * HEAD_SIZE, (g + 1) * HEAD_SIZE)
            merged.append(
                functools.reduce(
                    jnp.add,
                    [
                        share[:, g : g + 1] * block[:, columns].astype(F32)
                        for share, block in zip(shares, blocks)
                    ],
                ).astype(BF16)
            )
        merged.append(three_terms(spread_terms(highest + jnp.log2(whole))))
        return jnp.concatenate(merged, axis=1)

    def r_copy(i):
        peer = row_peer(row_offsets[i])
        return pltpu.make_async_remote_copy(
            src_ref=ret_out.at[pair_block(peer)],
            dst_ref=ret_in.at[pair_block(me)],
            send_sem=r_send.at[i],
            recv_sem=r_recv.at[i],
            device_id={"prompt": peer},
            device_id_type=MESH,
        )

    def finish_head():
        others = [ctx_peer(offset) for offset in ctx_offsets]
        for other in others:
            p_arrival(other).wait_recv()
        merged = merge([part_out[own_step]] + [part_in[other] for other in others])
        ret_out[...] = dot(back_table[...], merged).astype(BF16)
        for i in range(row_count - 1):
            r_copy(i).start()
        ret_in[pair_block(me), :] = ret_out[pair_block(me), :]

    def prefix_head(s):
        query = split_query(heads_q[step_head(s)])
        rows = query.shape[0]

        def scores_of(i):
            return dot_rows(query, twice(lead[s, i * chunk : (i + 1) * chunk, 0:HEAD_SIZE]))

        highest = jnp.full((rows, 1), -1e30, F32)
        total = jnp.zeros((rows, 2 * HEAD_SIZE), F32)
        scores = scores_of(0)
        for i in range(span // chunk):
            later = scores_of(i + 1) if (i + 1) * chunk < span else None
            top = jnp.maximum(highest, jnp.max(scores, axis=1, keepdims=True))
            weights = jnp.exp2(scores - top).astype(BF16)
            total = total * jnp.exp2(highest - top) + dot(
                weights, with_ones(lead[s, i * chunk : (i + 1) * chunk, HEAD_SIZE:])
            )
            highest, scores = top, later
        sums = total[:, HEAD_SIZE:]
        values = (total[:, :HEAD_SIZE] / sums).astype(BF16)
        for g in range(GROUP):
            part_out[s, :, g * HEAD_SIZE : (g + 1) * HEAD_SIZE] = values[g * ROWS : (g + 1) * ROWS, :]
        part_out[s, :, WIDTH:] = three_terms(by_group_lane(highest + jnp.log2(sums), ROWS, 3))

    def prefix_step(s, _):
        pl.when(s == core)(take_queries)
        lead_copy(s).wait()

        ahead = s + core

        @pl.when((step_core(ahead) == core) & (ahead != own_step))
        def _():
            handed = twin_copy(step_head(ahead))
            handed.wait_recv()
            handed.start()

        @pl.when(step_core(s) != core)
        def _():
            twin_copy(step_head(s)).wait_recv()

        prefix_head(s)

        @pl.when(s != own_step)
        def _():
            p_copy(s).start()

        @pl.when(s == 0)
        def _():
            lax.fori_loop(early, groups, suffix_group, 0)

        pl.when(s == FINISH_STEP + (ctx_count - 1 - FINISH_STEP) * core)(finish_head)
        return 0

    lax.fori_loop(0, ctx_count, prefix_step, 0)

    for i in range(row_count - 1):
        q_copy(i).wait_send()
    for i in range(len(near)):
        c_copy(i).wait_send()
    for k in range(1, x_count):
        twin_copy((x + k) % x_count * 2 + core).wait_send()
    for s in range(ctx_count):

        @pl.when(s != own_step)
        def _():
            p_copy(s).wait_send()

    for i in range(row_count - 1):
        r_copy(i).wait_recv()

    home = dot(home_table[...], ret_in[...])
    alive = jnp.sum(home_table[...].astype(F32), axis=1, keepdims=True)
    prefix_mass = sum_terms(home[:, WIDTH:])
    suffix_mass = suffix_lse[...]
    top = jnp.maximum(prefix_mass, suffix_mass)
    mass = top + jnp.log2(jnp.exp2(prefix_mass - top) + jnp.exp2(suffix_mass - top))
    prefix_share = jnp.exp2(prefix_mass - mass) * alive
    suffix_share = jnp.exp2(suffix_mass - mass) * alive
    for g in range(GROUP):
        columns = slice(g * HEAD_SIZE, (g + 1) * HEAD_SIZE)
        mixed = (
            prefix_share[:, g : g + 1] * home[:, columns] + suffix_share[:, g : g + 1] * suffix[:, columns]
        )
        out_ref[:, :, columns] = mixed.reshape(OWNER_SLOTS, STEPS, HEAD_SIZE).astype(BF16)
    terms = three_terms(spread_terms(mass * (alive * LN2)))
    by_step = one_hot(
        (iota((SLOT_ROWS, SLOT_ROWS), 0) % STEPS == iota((SLOT_ROWS, SLOT_ROWS), 1) // OWNER_SLOTS)
        & (iota((SLOT_ROWS, SLOT_ROWS), 0) // STEPS == iota((SLOT_ROWS, SLOT_ROWS), 1) % OWNER_SLOTS)
    ).astype(BF16)
    turned = lax.dot_general(terms, by_step, (((0,), (0,)), ((), ())), preferred_element_type=F32)
    turned = turned[:GROUP] + turned[GROUP : 2 * GROUP] + turned[2 * GROUP : 3 * GROUP]
    for t in range(STEPS):
        mass_ref[t] = turned[:, t * OWNER_SLOTS : (t + 1) * OWNER_SLOTS]

    for i in range(row_count - 1):
        r_copy(i).wait_send()


def hand_over(attended, mass, attended_out, mass_out):
    attended_out[...] = attended[...]
    mass_out[...] = mass[...]


def per_device(probe_vectors, tail_memory, lead_memory, active_rollouts, holder_map, tail_fill):
    row_count = lax.axis_size("prompt")
    ctx_count = lax.axis_size("ctx")
    slots, steps, width = probe_vectors.shape
    span = lead_memory.shape[1]
    tail_span = tail_memory.shape[1]
    pairs = row_count * PAIR_ROWS
    vmem = pl.BlockSpec(memory_space=pltpu.VMEM)
    anywhere = pl.BlockSpec(memory_space=pl.ANY)
    dma = pltpu.SemaphoreType.DMA
    attended, log_mass = pl.pallas_call(
        kernel,
        out_shape=(
            jax.ShapeDtypeStruct((slots, steps, width), BF16),
            jax.ShapeDtypeStruct((steps, GROUP, slots), F32),
        ),
        in_specs=[anywhere] * 6,
        out_specs=(vmem, vmem),
        scratch_shapes=[
            pltpu.VMEM((slots, steps, width), BF16),
            pltpu.VMEM((1, active_rollouts.shape[0]), jnp.int32),
            pltpu.VMEM((1, holder_map.shape[0]), jnp.int32),
            pltpu.VMEM((1, slots), jnp.int32),
            pltpu.VMEM((slots, tail_span, 2 * HEAD_SIZE), BF16),
            pltpu.VMEM((ctx_count, span, 2 * HEAD_SIZE), BF16),
            pltpu.VMEM((SLOT_ROWS, WIDTH), BF16),
            pltpu.VMEM((pairs, WIDTH), BF16),
            pltpu.VMEM((pairs, WIDTH), BF16),
            pltpu.VMEM((ctx_count, ROWS, WIDTH), BF16),
            pltpu.VMEM((ctx_count, ROWS, PAYLOAD), BF16),
            pltpu.VMEM((ctx_count, ROWS, PAYLOAD), BF16),
            pltpu.VMEM((pairs, PAYLOAD), BF16),
            pltpu.VMEM((pairs, PAYLOAD), BF16),
            pltpu.VMEM((SLOT_ROWS, WIDTH), F32),
            pltpu.VMEM((SLOT_ROWS, 128), F32),
            pltpu.VMEM((ROWS, pairs), BF16),
            pltpu.VMEM((pairs, ROWS), BF16),
            pltpu.VMEM((SLOT_ROWS, pairs), BF16),
            dma((4,)),
            dma,
            dma((ctx_count,)),
            dma((row_count,)),
            dma((row_count,)),
            dma((ctx_count,)),
            dma((ctx_count,)),
            dma((ctx_count // 2,)),
            dma((ctx_count,)),
            dma((ctx_count,)),
            dma((row_count,)),
            dma((row_count,)),
        ],
        compiler_params=pltpu.CompilerParams(
            collective_id=0, has_side_effects=True, vmem_limit_bytes=56 * 2**20
        ),
        cost_estimate=pl.CostEstimate(
            flops=5_000_000_000, bytes_accessed=22_000_000, transcendentals=9_000_000
        ),
        name="grouped_attention",
    )(
        probe_vectors,
        active_rollouts.reshape(1, -1),
        holder_map.reshape(1, -1),
        tail_fill.reshape(1, -1),
        tail_memory,
        lead_memory.reshape(span, -1),
    )
    attended, log_mass = pl.pallas_call(
        hand_over,
        out_shape=(
            jax.ShapeDtypeStruct(attended.shape, attended.dtype),
            jax.ShapeDtypeStruct(log_mass.shape, log_mass.dtype),
        ),
        in_specs=[vmem, vmem],
        out_specs=(vmem, vmem),
        name="hand_over",
    )(attended, log_mass)
    return attended, jnp.transpose(log_mass, (2, 0, 1))


def solution(mesh):
    return jax.shard_map(
        per_device,
        mesh=mesh,
        in_specs=(
            P("prompt", None, "ctx"),
            P("prompt", None, "ctx"),
            P("prompt", "ctx", None),
            P(),
            P(),
            P("prompt"),
        ),
        out_specs=(P("prompt", None, "ctx"), P("prompt", None, "ctx")),
        check_vma=False,
    )
```

```python
import functools

import jax
import jax.numpy as jnp
from jax import lax
from jax.experimental import pallas as pl
from jax.experimental.pallas import tpu as pltpu
from jax.sharding import PartitionSpec as P

QUERY_HEADS = 64
KEY_VALUE_HEADS = 8
HEAD_SIZE = 128
SAMPLE_COUNT = 8
CAP = 4
OWNER_SLOTS = 16
STEPS = 4
GROUP = QUERY_HEADS // KEY_VALUE_HEADS
WIDTH = GROUP * HEAD_SIZE
PAYLOAD = WIDTH + 128
ROWS = SAMPLE_COUNT * STEPS
SLOT_ROWS = OWNER_SLOTS * STEPS
PAIR_ROWS = CAP * STEPS
CHUNK = 1024
EARLY_GROUPS = 3
FINISH_STEP = 6
LOG2E = 1.4426950408889634
LN2 = 0.6931471805599453
SCALE = HEAD_SIZE**-0.5 * LOG2E
F32 = jnp.float32
BF16 = jnp.bfloat16
MESH = pl.DeviceIdType.MESH


def iota(shape, dim):
    return lax.broadcasted_iota(jnp.int32, shape, dim)


def one_hot(condition):
    return jnp.where(condition, 1.0, 0.0).astype(F32)


def dot(a, b):
    return jnp.dot(a, b, preferred_element_type=F32)


def dot_rows(a, b):
    return lax.dot_general(a, b, (((1,), (1,)), ((), ())), preferred_element_type=F32)


def layout_vectors(active, holder):
    count = holder.shape[1]
    rows, lanes = iota((count, count), 0), iota((count, count), 1)
    diagonal = rows == lanes
    owner_row = holder.astype(F32)
    owner_col = jnp.sum(jnp.where(diagonal, owner_row, 0.0), axis=1, keepdims=True)
    prompts = active.shape[1]
    in_prompt = iota((count, prompts), 0) // SAMPLE_COUNT == iota((count, prompts), 1)
    kept = jnp.sum(jnp.where(in_prompt, active.astype(F32), 0.0), axis=1, keepdims=True)
    live_col = one_hot((iota((count, 1), 0) % SAMPLE_COUNT).astype(F32) < kept)
    live_row = jnp.sum(jnp.where(diagonal, live_col, 0.0), axis=0, keepdims=True)
    same_owner = owner_col == owner_row
    same_prompt = rows // SAMPLE_COUNT == lanes // SAMPLE_COUNT
    before_row = jnp.where(same_owner & (rows < lanes), live_col, 0.0)
    before_col = jnp.where(same_owner & (lanes < rows), live_row, 0.0)
    slot_row = jnp.sum(before_row, axis=0, keepdims=True)
    slot_col = jnp.sum(before_col, axis=1, keepdims=True)
    ordinal_row = jnp.sum(jnp.where(same_prompt, before_row, 0.0), axis=0, keepdims=True)
    ordinal_col = jnp.sum(jnp.where(same_prompt, before_col, 0.0), axis=1, keepdims=True)
    return (owner_row, live_row, slot_row, ordinal_row), (owner_col, live_col, slot_col, ordinal_col)


def same_step(rows, columns):
    return iota((rows, columns), 0) % STEPS == iota((rows, columns), 1) % STEPS


def split_query(block):
    scaled = block.astype(F32) * SCALE
    high = scaled.astype(BF16)
    low = (scaled - high.astype(F32)).astype(BF16)
    pieces = [
        jnp.concatenate(
            [high[:, g * HEAD_SIZE : (g + 1) * HEAD_SIZE], low[:, g * HEAD_SIZE : (g + 1) * HEAD_SIZE]],
            axis=1,
        )
        for g in range(GROUP)
    ]
    return jnp.concatenate(pieces, axis=0)


def twice(keys):
    return jnp.concatenate([keys, keys], axis=1)


def with_ones(values):
    return jnp.concatenate([values, jnp.ones_like(values)], axis=1)


def by_group_lane(column_blocks, rows, copies):
    lane = iota((rows, 128), 1)
    out = jnp.zeros((rows, 128), F32)
    for g in range(GROUP):
        here = (lane % GROUP == g) & (lane < copies * GROUP)
        out = jnp.where(here, column_blocks[g * rows : (g + 1) * rows, :], out)
    return out


def three_terms(value):
    lane = iota(value.shape, 1)
    high = value.astype(BF16).astype(F32)
    rest = value - high
    middle = rest.astype(BF16).astype(F32)
    low = rest - middle
    out = jnp.where(lane < GROUP, high, jnp.where(lane < 2 * GROUP, middle, low))
    return jnp.where(lane < 3 * GROUP, out, 0.0).astype(BF16)


def sum_terms(terms):
    value = terms.astype(F32)
    return value + pltpu.roll(value, 128 - GROUP, 1) + pltpu.roll(value, 128 - 2 * GROUP, 1)


def spread_terms(value):
    lane = iota(value.shape, 1)
    return jnp.where(
        lane < GROUP,
        value,
        jnp.where(lane < 2 * GROUP, pltpu.roll(value, GROUP, 1), pltpu.roll(value, 2 * GROUP, 1)),
    )


def kernel(
    probes_hbm,
    active_hbm,
    holder_hbm,
    fill_hbm,
    tail_hbm,
    lead_hbm,
    ret_in,
    suffix_hbm,
    suffix_lse_hbm,
    home_table_hbm,
    probes,
    active,
    holder,
    fill,
    tail,
    lead,
    queries,
    send_q,
    recv_q,
    heads_q,
    part_out,
    part_in,
    ret_out,
    suffix,
    suffix_lse,
    take_table,
    back_table,
    home_table,
    small_sem,
    tail_sem,
    lead_sem,
    q_send,
    q_recv,
    c_send,
    c_recv,
    t_send,
    p_send,
    p_recv,
    r_send,
    r_recv,
    own_sem,
    home_sem,
):
    row_count = lax.axis_size("prompt")
    ctx_count = lax.axis_size("ctx")
    x_count = ctx_count // 2
    y_count = min(4, row_count)
    z_count = row_count // y_count
    me = lax.axis_index("prompt")
    ctx = lax.axis_index("ctx")
    x, core = lax.div(ctx, 2), lax.rem(ctx, 2)
    z, y = lax.div(me, y_count), lax.rem(me, y_count)
    span = lead_hbm.shape[0]
    chunk = min(CHUNK, span)
    pairs = row_count * PAIR_ROWS

    def ring(a, size):
        return min(a, size - a)

    row_offsets = sorted(
        [(a, b) for a in range(z_count) for b in range(y_count) if a or b],
        key=lambda ab: -ring(ab[0], z_count) - ring(ab[1], y_count),
    )
    ctx_offsets = sorted(
        [(a, b) for a in range(x_count) for b in range(2) if a or b],
        key=lambda ab: -2 * ring(ab[0], x_count) - ab[1],
    )

    def row_peer(offset):
        return lax.rem(z + offset[0], z_count) * y_count + lax.rem(y + offset[1], y_count)

    def ctx_peer(offset):
        return lax.rem(x + offset[0], x_count) * 2 + lax.rem(core + offset[1], 2)

    def pair_block(index):
        return pl.ds(pl.multiple_of(index * PAIR_ROWS, PAIR_ROWS), PAIR_ROWS)

    barrier = pltpu.get_barrier_semaphore()
    for offset in row_offsets:
        pl.semaphore_signal(barrier, inc=1, device_id={"prompt": row_peer(offset)}, device_id_type=MESH)
    for offset in ctx_offsets:
        pl.semaphore_signal(barrier, inc=1, device_id={"ctx": ctx_peer(offset)}, device_id_type=MESH)

    small_copies = [
        pltpu.make_async_copy(source, target, small_sem.at[i])
        for i, (source, target) in enumerate(
            [(active_hbm, active), (holder_hbm, holder), (probes_hbm, probes), (fill_hbm, fill)]
        )
    ]
    for copy in small_copies:
        copy.start()

    def step_x(s):
        return lax.rem(x + lax.rem(s, x_count) + lax.div(s, x_count), x_count)

    def step_core(s):
        return lax.div(s, x_count)

    def step_head(s):
        return step_x(s) * 2 + step_core(s)

    own_step = core * (ctx_count - 1)
    tail_copy = pltpu.make_async_copy(tail_hbm, tail, tail_sem)
    tail_copy.start()

    def lead_copy(s):
        first = pl.multiple_of(step_head(s) * 2 * HEAD_SIZE, 2 * HEAD_SIZE)
        return pltpu.make_async_copy(
            lead_hbm.at[:, pl.ds(first, 2 * HEAD_SIZE)], lead.at[s], lead_sem.at[s]
        )

    def start_lead(s, _):
        lead_copy(s).start()
        return 0

    lax.fori_loop(0, ctx_count, start_lead, 0)

    for copy in small_copies:
        copy.wait()

    row_form, col_form = layout_vectors(active[...], holder[...])
    owner_row, live_row, slot_row, ordinal_row = row_form
    owner_col, live_col, slot_col, ordinal_col = col_form
    count = owner_row.shape[1]
    my_row = me.astype(F32)

    pair_of_row = iota((pairs, count), 0) // STEPS
    pair_of_col = iota((count, pairs), 1) // STEPS
    sample_of_lane = iota((pairs, count), 1)
    sample_of_row = iota((count, pairs), 0)
    mine_row = live_row * one_hot(owner_row == my_row)
    to_pair = jnp.where(
        (pair_of_row // CAP == sample_of_lane // SAMPLE_COUNT)
        & ((pair_of_row % CAP).astype(F32) == ordinal_row),
        mine_row,
        0.0,
    )
    from_slot = one_hot((iota((count, SLOT_ROWS), 1) // STEPS).astype(F32) == slot_col)
    send_table = jnp.where(
        same_step(pairs, SLOT_ROWS), dot(to_pair.astype(BF16), from_slot.astype(BF16)), 0.0
    ).astype(BF16)
    queries[...] = probes[...].astype(F32).reshape(SLOT_ROWS, WIDTH).astype(BF16)
    send_q[...] = dot(send_table, queries[...]).astype(BF16)

    pl.semaphore_wait(barrier, row_count - 1 + ctx_count - 1)

    def q_copy(i):
        peer = row_peer(row_offsets[i])
        return pltpu.make_async_remote_copy(
            src_ref=send_q.at[pair_block(peer)],
            dst_ref=recv_q.at[pair_block(me)],
            send_sem=q_send.at[i],
            recv_sem=q_recv.at[i],
            device_id={"prompt": peer},
            device_id_type=MESH,
        )

    def start_q():
        for i in range(row_count - 1):
            q_copy(i).start()

    pl.when(core == 0)(start_q)
    recv_q[pair_block(me), :] = send_q[pair_block(me), :]

    as_sample = jnp.where(
        (iota((ROWS, count), 1) // SAMPLE_COUNT == me)
        & (iota((ROWS, count), 1) % SAMPLE_COUNT == iota((ROWS, count), 0) // STEPS),
        live_row,
        0.0,
    )
    at_pair = one_hot(
        ((pair_of_col // CAP).astype(F32) == owner_col) & ((pair_of_col % CAP).astype(F32) == ordinal_col)
    )
    take_table[...] = jnp.where(
        same_step(ROWS, pairs), dot(as_sample.astype(BF16), at_pair.astype(BF16)), 0.0
    ).astype(BF16)
    of_pair = one_hot(
        ((pair_of_row // CAP).astype(F32) == owner_row) & ((pair_of_row % CAP).astype(F32) == ordinal_row)
    )
    of_sample = jnp.where(
        (iota((count, ROWS), 0) // SAMPLE_COUNT == me)
        & (iota((count, ROWS), 0) % SAMPLE_COUNT == iota((count, ROWS), 1) // STEPS),
        live_col,
        0.0,
    )
    back_table[...] = jnp.where(
        same_step(pairs, ROWS), dot(of_pair.astype(BF16), of_sample.astype(BF16)), 0.0
    ).astype(BF16)
    mine_col = live_col * one_hot(owner_col == my_row)
    into_slot = one_hot((iota((SLOT_ROWS, count), 0) // STEPS).astype(F32) == slot_row)
    from_pair = jnp.where(
        (pair_of_col // CAP == sample_of_row // SAMPLE_COUNT)
        & ((pair_of_col % CAP).astype(F32) == ordinal_col),
        mine_col,
        0.0,
    )
    home_table[...] = jnp.where(
        same_step(SLOT_ROWS, pairs), dot(into_slot.astype(BF16), from_pair.astype(BF16)), 0.0
    ).astype(BF16)

    tail_copy.wait()
    batch = 4
    block_rows = batch * STEPS
    tail_rows = GROUP * block_rows
    tail_span = tail.shape[1]

    home_copies = [
        pltpu.make_async_copy(source, target, home_sem.at[i])
        for i, (source, target) in enumerate(
            [(suffix, suffix_hbm), (suffix_lse, suffix_lse_hbm), (home_table, home_table_hbm)]
        )
    ]

    def suffix_group(q, _):
        rows = pl.ds(pl.multiple_of(q * block_rows, block_rows), block_rows)
        query = split_query(queries[rows, :])
        row = iota((tail_rows, 1), 0)
        which = (row // STEPS) % batch
        scores = jnp.zeros((tail_rows, tail_span), F32)
        for s in range(batch):
            found = dot_rows(query, twice(tail[q * batch + s, :, 0:HEAD_SIZE]))
            scores = jnp.where(which == s, found, scores)
        filled = jnp.sum(
            jnp.where(
                iota((tail_rows, OWNER_SLOTS), 1) == q * batch + which, fill[...].astype(F32), 0.0
            ),
            axis=1,
            keepdims=True,
        )
        limit = filled - (STEPS - 1) + (row % STEPS).astype(F32)
        visible = iota((tail_rows, tail_span), 1).astype(F32) < limit
        scores = jnp.where(visible, scores, -1e30)
        highest = jnp.max(scores, axis=1, keepdims=True)
        weights = jnp.exp2(scores - highest).astype(BF16)
        total = jnp.zeros((tail_rows, 2 * HEAD_SIZE), F32)
        for s in range(batch):
            found = dot(weights, with_ones(tail[q * batch + s, :, HEAD_SIZE:]))
            total = jnp.where(which == s, found, total)
        sums = total[:, HEAD_SIZE:]
        values = total[:, :HEAD_SIZE] / sums
        for g in range(GROUP):
            suffix[rows, g * HEAD_SIZE : (g + 1) * HEAD_SIZE] = values[
                g * block_rows : (g + 1) * block_rows, :
            ]
        suffix_lse[rows, :] = by_group_lane(highest + jnp.log2(sums), block_rows, 1)
        return 0

    groups = OWNER_SLOTS // batch
    early = EARLY_GROUPS + (groups - EARLY_GROUPS) * core
    lax.fori_loop(0, early, suffix_group, 0)
    pl.when(core == 1)(start_q)

    near = [(0, 1)] + [(x_count - k, 0) for k in range(1, x_count)]

    def c_copy(i):
        return pltpu.make_async_remote_copy(
            src_ref=heads_q.at[ctx],
            dst_ref=heads_q.at[ctx],
            send_sem=c_send.at[i],
            recv_sem=c_recv.at[ctx],
            device_id={"ctx": ctx_peer(near[i])},
            device_id_type=MESH,
        )

    def twin_copy(head):
        return pltpu.make_async_remote_copy(
            src_ref=heads_q.at[head],
            dst_ref=heads_q.at[head],
            send_sem=t_send.at[head // 2],
            recv_sem=c_recv.at[head],
            device_id={"ctx": ctx_peer((0, 1))},
            device_id_type=MESH,
        )

    def take_queries():
        for i in range(row_count - 1):
            q_copy(i).wait_recv()
        heads_q[ctx] = dot(take_table[...], recv_q[...]).astype(BF16)
        for i in range(len(near)):
            c_copy(i).start()

    def p_copy(s):
        return pltpu.make_async_remote_copy(
            src_ref=part_out.at[s],
            dst_ref=part_in.at[ctx],
            send_sem=p_send.at[s],
            recv_sem=p_recv.at[ctx],
            device_id={"ctx": step_head(s)},
            device_id_type=MESH,
        )

    def p_arrival(source):
        return pltpu.make_async_remote_copy(
            src_ref=part_out.at[0],
            dst_ref=part_in.at[source],
            send_sem=p_send.at[0],
            recv_sem=p_recv.at[source],
            device_id={"ctx": source},
            device_id_type=MESH,
        )

    def merge(blocks):
        masses = [sum_terms(block[:, WIDTH:]) for block in blocks]
        highest = functools.reduce(jnp.maximum, masses)
        shares = [jnp.exp2(mass - highest) for mass in masses]
        whole = functools.reduce(jnp.add, shares)
        shares = [share / whole for share in shares]
        merged = []
        for g in range(GROUP):
            columns = slice(g * HEAD_SIZE, (g + 1) * HEAD_SIZE)
            merged.append(
                functools.reduce(
                    jnp.add,
                    [
                        share[:, g : g + 1] * block[:, columns].astype(F32)
                        for share, block in zip(shares, blocks)
                    ],
                ).astype(BF16)
            )
        merged.append(three_terms(spread_terms(highest + jnp.log2(whole))))
        return jnp.concatenate(merged, axis=1)

    def r_copy(i):
        peer = row_peer(row_offsets[i])
        return pltpu.make_async_remote_copy(
            src_ref=ret_out.at[pair_block(peer)],
            dst_ref=ret_in.at[pair_block(me)],
            send_sem=r_send.at[i],
            recv_sem=r_recv.at[i],
            device_id={"prompt": peer},
            device_id_type=MESH,
        )

    def own_copy():
        return pltpu.make_async_copy(ret_out.at[pair_block(me)], ret_in.at[pair_block(me)], own_sem)

    def finish_head():
        others = [ctx_peer(offset) for offset in ctx_offsets]
        for other in others:
            p_arrival(other).wait_recv()
        merged = merge([part_out[own_step]] + [part_in[other] for other in others])
        ret_out[...] = dot(back_table[...], merged).astype(BF16)
        for i in range(row_count - 1):
            r_copy(i).start()
        own_copy().start()

    def prefix_head(s):
        query = split_query(heads_q[step_head(s)])
        rows = query.shape[0]

        def scores_of(i):
            return dot_rows(query, twice(lead[s, i * chunk : (i + 1) * chunk, 0:HEAD_SIZE]))

        highest = jnp.full((rows, 1), -1e30, F32)
        total = jnp.zeros((rows, 2 * HEAD_SIZE), F32)
        scores = scores_of(0)
        for i in range(span // chunk):
            later = scores_of(i + 1) if (i + 1) * chunk < span else None
            top = jnp.maximum(highest, jnp.max(scores, axis=1, keepdims=True))
            weights = jnp.exp2(scores - top).astype(BF16)
            total = total * jnp.exp2(highest - top) + dot(
                weights, with_ones(lead[s, i * chunk : (i + 1) * chunk, HEAD_SIZE:])
            )
            highest, scores = top, later
        sums = total[:, HEAD_SIZE:]
        values = (total[:, :HEAD_SIZE] / sums).astype(BF16)
        for g in range(GROUP):
            part_out[s, :, g * HEAD_SIZE : (g + 1) * HEAD_SIZE] = values[g * ROWS : (g + 1) * ROWS, :]
        part_out[s, :, WIDTH:] = three_terms(by_group_lane(highest + jnp.log2(sums), ROWS, 3))

    def prefix_step(s, _):
        pl.when(s == core)(take_queries)
        lead_copy(s).wait()

        ahead = s + core

        @pl.when((step_core(ahead) == core) & (ahead != own_step))
        def _():
            handed = twin_copy(step_head(ahead))
            handed.wait_recv()
            handed.start()

        @pl.when(step_core(s) != core)
        def _():
            twin_copy(step_head(s)).wait_recv()

        prefix_head(s)

        @pl.when(s != own_step)
        def _():
            p_copy(s).start()

        @pl.when(s == 0)
        def _():
            lax.fori_loop(early, groups, suffix_group, 0)
            for copy in home_copies:
                copy.start()

        pl.when(s == FINISH_STEP + (ctx_count - 1 - FINISH_STEP) * core)(finish_head)
        return 0

    lax.fori_loop(0, ctx_count, prefix_step, 0)

    for i in range(row_count - 1):
        q_copy(i).wait_send()
    for i in range(len(near)):
        c_copy(i).wait_send()
    for k in range(1, x_count):
        twin_copy((x + k) % x_count * 2 + core).wait_send()
    for s in range(ctx_count):

        @pl.when(s != own_step)
        def _():
            p_copy(s).wait_send()

    for i in range(row_count - 1):
        r_copy(i).wait_recv()
    own_copy().wait()
    for copy in home_copies:
        copy.wait()

    for i in range(row_count - 1):
        r_copy(i).wait_send()


def home_kernel(arrived, home_table, suffix, suffix_lse, out_ref, mass_ref):
    table = home_table[...]
    home = dot(table, arrived[...])
    alive = jnp.sum(table.astype(F32), axis=1, keepdims=True)
    prefix_mass = sum_terms(home[:, WIDTH:])
    suffix_mass = suffix_lse[...]
    top = jnp.maximum(prefix_mass, suffix_mass)
    mass = top + jnp.log2(jnp.exp2(prefix_mass - top) + jnp.exp2(suffix_mass - top))
    prefix_share = jnp.exp2(prefix_mass - mass) * alive
    suffix_share = jnp.exp2(suffix_mass - mass) * alive
    for g in range(GROUP):
        columns = slice(g * HEAD_SIZE, (g + 1) * HEAD_SIZE)
        mixed = (
            prefix_share[:, g : g + 1] * home[:, columns] + suffix_share[:, g : g + 1] * suffix[:, columns]
        )
        out_ref[:, :, columns] = mixed.reshape(OWNER_SLOTS, STEPS, HEAD_SIZE).astype(BF16)
    terms = three_terms(spread_terms(mass * (alive * LN2)))
    by_step = one_hot(
        (iota((SLOT_ROWS, SLOT_ROWS), 0) % STEPS == iota((SLOT_ROWS, SLOT_ROWS), 1) // OWNER_SLOTS)
        & (iota((SLOT_ROWS, SLOT_ROWS), 0) // STEPS == iota((SLOT_ROWS, SLOT_ROWS), 1) % OWNER_SLOTS)
    ).astype(BF16)
    turned = lax.dot_general(terms, by_step, (((0,), (0,)), ((), ())), preferred_element_type=F32)
    turned = turned[:GROUP] + turned[GROUP : 2 * GROUP] + turned[2 * GROUP : 3 * GROUP]
    for t in range(STEPS):
        mass_ref[t] = turned[:, t * OWNER_SLOTS : (t + 1) * OWNER_SLOTS]


def per_device(probe_vectors, tail_memory, lead_memory, active_rollouts, holder_map, tail_fill):
    row_count = lax.axis_size("prompt")
    ctx_count = lax.axis_size("ctx")
    slots, steps, width = probe_vectors.shape
    span = lead_memory.shape[1]
    tail_span = tail_memory.shape[1]
    pairs = row_count * PAIR_ROWS
    vmem = pl.BlockSpec(memory_space=pltpu.VMEM)
    anywhere = pl.BlockSpec(memory_space=pl.ANY)
    dma = pltpu.SemaphoreType.DMA
    arrived, suffix, suffix_lse, home_table = pl.pallas_call(
        kernel,
        out_shape=(
            jax.ShapeDtypeStruct((pairs, PAYLOAD), BF16),
            jax.ShapeDtypeStruct((SLOT_ROWS, WIDTH), F32),
            jax.ShapeDtypeStruct((SLOT_ROWS, 128), F32),
            jax.ShapeDtypeStruct((SLOT_ROWS, pairs), BF16),
        ),
        in_specs=[anywhere] * 6,
        out_specs=(anywhere,) * 4,
        scratch_shapes=[
            pltpu.VMEM((slots, steps, width), BF16),
            pltpu.VMEM((1, active_rollouts.shape[0]), jnp.int32),
            pltpu.VMEM((1, holder_map.shape[0]), jnp.int32),
            pltpu.VMEM((1, slots), jnp.int32),
            pltpu.VMEM((slots, tail_span, 2 * HEAD_SIZE), BF16),
            pltpu.VMEM((ctx_count, span, 2 * HEAD_SIZE), BF16),
            pltpu.VMEM((SLOT_ROWS, WIDTH), BF16),
            pltpu.VMEM((pairs, WIDTH), BF16),
            pltpu.VMEM((pairs, WIDTH), BF16),
            pltpu.VMEM((ctx_count, ROWS, WIDTH), BF16),
            pltpu.VMEM((ctx_count, ROWS, PAYLOAD), BF16),
            pltpu.VMEM((ctx_count, ROWS, PAYLOAD), BF16),
            pltpu.VMEM((pairs, PAYLOAD), BF16),
            pltpu.VMEM((SLOT_ROWS, WIDTH), F32),
            pltpu.VMEM((SLOT_ROWS, 128), F32),
            pltpu.VMEM((ROWS, pairs), BF16),
            pltpu.VMEM((pairs, ROWS), BF16),
            pltpu.VMEM((SLOT_ROWS, pairs), BF16),
            dma((4,)),
            dma,
            dma((ctx_count,)),
            dma((row_count,)),
            dma((row_count,)),
            dma((ctx_count,)),
            dma((ctx_count,)),
            dma((ctx_count // 2,)),
            dma((ctx_count,)),
            dma((ctx_count,)),
            dma((row_count,)),
            dma((row_count,)),
            dma,
            dma((3,)),
        ],
        compiler_params=pltpu.CompilerParams(
            collective_id=0, has_side_effects=True, vmem_limit_bytes=56 * 2**20
        ),
        cost_estimate=pl.CostEstimate(
            flops=5_000_000_000, bytes_accessed=22_000_000, transcendentals=9_000_000
        ),
        name="grouped_attention",
    )(
        probe_vectors,
        active_rollouts.reshape(1, -1),
        holder_map.reshape(1, -1),
        tail_fill.reshape(1, -1),
        tail_memory,
        lead_memory.reshape(span, -1),
    )
    attended, log_mass = pl.pallas_call(
        home_kernel,
        out_shape=(
            jax.ShapeDtypeStruct((slots, steps, width), BF16),
            jax.ShapeDtypeStruct((steps, GROUP, slots), F32),
        ),
        in_specs=[vmem] * 4,
        out_specs=(vmem, vmem),
        name="home_rows",
    )(arrived, home_table, suffix, suffix_lse)
    return attended, jnp.transpose(log_mass, (2, 0, 1))


def solution(mesh):
    return jax.shard_map(
        per_device,
        mesh=mesh,
        in_specs=(
            P("prompt", None, "ctx"),
            P("prompt", None, "ctx"),
            P("prompt", "ctx", None),
            P(),
            P(),
            P("prompt"),
        ),
        out_specs=(P("prompt", None, "ctx"), P("prompt", None, "ctx")),
        check_vma=False,
    )
```
